256 devices in a mesh: ctx: 64 (over z, y, x_lo), fsdp: 4 (over x_hi, core).
Axes of the slice: x: 4 (x_hi: 2, x_lo: 2; x = x_hi * 2 + x_lo), y: 4, z: 8, core: 2. Of those that a mesh axis runs over, the one named last changes fastest.
Arguments:
- video_query: bfloat16 [4, 32768, 1024], P('fsdp', 'ctx'), may hold values from -256 to 256
- audio_key: bfloat16 [4, 512, 1024], P('fsdp', 'ctx'), may hold values from -9 to 9
- audio_value: bfloat16 [4, 512, 1024], P('fsdp', 'ctx'), may hold values from -6 to 6
- out_weight: bfloat16 [1024, 4096], P(None, 'fsdp'), may hold values from -0.1875 to 0.1875
- grad_out: bfloat16 [4, 32768, 4096], P('fsdp', 'ctx'), may hold values from -6 to 6
- query_time: int32 [32768], P('ctx'), may hold values from 0 to 511, as said below
- window: int32 [2, 32768], P(None, 'ctx'), may hold values from 0 to 512, as said below
Outputs:
- output: bfloat16 [4, 32768, 4096], P('fsdp', 'ctx')
- query_grad: bfloat16 [4, 32768, 1024], P('fsdp', 'ctx')
- key_grad: float32 [4, 512, 1024], P('fsdp', 'ctx')
- value_grad: float32 [4, 512, 1024], P('fsdp', 'ctx')
- weight_grad: float32 [1024, 4096], P('ctx', 'fsdp')
The draws below stay inside these ranges and needn't reach their ends.
Inputs may be any that keep to these rules, and one draw needn't show every extreme that they name: query_time of video token i lies in [window[0, i], window[1, i]). For video token i, with d = i // 512: max(0, (d - 1) * 8) <= window[0, i] < window[1, i] <= min(512, (d + 2) * 8); both bounds are reached by some token of every d.
All inputs are finite; a program needn't handle non-finite values.
Results may differ from the reference program's by a relative error of at most 0.027.
The reference program's roundings to bfloat16 on the way (of `query_rot`, `key_rot`, `probs_low`, `attended`, `att_grad` and `score_grad`) count: a program that leaves them out, or rounds other values in their place, can miss the bound.
Values may be sent and summed in bfloat16 or wider, within the bound.
A program may use at most 128 MiB of HBM per device.

```python
import math
import jax
import jax.numpy as jnp
from jax import lax

D = 4096
DH = 64
VTOK_DEV = 512
ATOK_DEV = 8
HD = 1024
CLIPS = 4
NV = 32768
NA = 512
N_CTX = 64


def alignment(key):
    base_key = jax.random.fold_in(key, 101)
    index = jnp.arange(NV, dtype=jnp.int32)
    shard = index // VTOK_DEV
    inside = index % VTOK_DEV
    centre = shard * ATOK_DEV + inside * ATOK_DEV // VTOK_DEV
    jitter = jax.random.randint(jax.random.fold_in(base_key, 1), (NV,), -(ATOK_DEV // 8), ATOK_DEV // 8 + 1)
    centre = jnp.clip(centre + jitter, shard * ATOK_DEV, shard * ATOK_DEV + ATOK_DEV - 1)
    centre = jnp.where(inside == 0, shard * ATOK_DEV, centre)
    centre = jnp.where(inside == VTOK_DEV - 1, shard * ATOK_DEV + ATOK_DEV - 1, centre)
    reach_low = jax.random.randint(jax.random.fold_in(base_key, 2), (NV,), ATOK_DEV // 4, ATOK_DEV + 1)
    reach_low = jnp.where(inside == 0, ATOK_DEV, reach_low)
    reach_high = jax.random.randint(jax.random.fold_in(base_key, 3), (NV,), ATOK_DEV // 4, ATOK_DEV + 1)
    reach_high = jnp.where(inside == VTOK_DEV - 1, ATOK_DEV, reach_high)
    lower = jnp.maximum(centre - reach_low, 0)
    upper = jnp.minimum(centre + 1 + reach_high, NA)
    return (centre.astype(jnp.int32), jnp.stack([lower, upper]).astype(jnp.int32))


def shared_keys(key):
    base_key = jax.random.fold_in(key, 201)
    keys = jax.random.truncated_normal(base_key, -6.0, 6.0, (CLIPS, NA, HD), jnp.float32)
    return keys


def draw_video_query(key, part):
    key = jax.random.fold_in(key, 7)
    values = jax.random.truncated_normal(jax.random.fold_in(key, 1), -6.0, 6.0, (CLIPS, NV, HD), jnp.float32)
    return values.astype(jnp.bfloat16)


def draw_audio_key(key, part):
    keys = shared_keys(key)
    return keys.astype(jnp.bfloat16)


def draw_query_time(key, part):
    centre, bounds = alignment(key)
    return centre


def draw_window(key, part):
    centre, bounds = alignment(key)
    return bounds


def levels(stream_key, dims, split, low, high):
    def one(dim, parts):
        steps = jax.random.uniform(jax.random.fold_in(jax.random.fold_in(stream_key, 6), dim), (parts,), jnp.float32, low / len(split), high / len(split))
        return jnp.repeat(jnp.exp(steps), dims[dim] // parts).reshape((-1,) + (1,) * (len(dims) - dim - 1))

    loudness = one(*split[0])
    for cut in split[1:]:
        loudness = loudness * one(*cut)
    return loudness


def bell_draw(key, extent, spread, reach, pieces=(), kind=jnp.bfloat16):
    drawn = jax.random.normal(key, extent, jnp.float32) * spread
    if len(pieces) > 0:
        drawn = levels(key, extent, pieces, -0.22, 0.18) * drawn
    return jnp.clip(drawn, min=-reach, max=reach).astype(kind)


def setup_inputs(seed: int = 0) -> dict:
    key_list = jax.random.split(jax.random.key(seed), 8)
    video_query = draw_video_query(jax.random.fold_in(key_list[7], 71), 0)
    audio_key = draw_audio_key(jax.random.fold_in(key_list[7], 71), 0)
    audio_value = bell_draw(key_list[2], (CLIPS, NA, HD), 1.0, 6.0, ((0, 4), (1, 64)))
    out_weight = bell_draw(key_list[3], (HD, D), HD ** -0.5, 0.1875, ((1, 4),))
    grad_out = bell_draw(key_list[4], (CLIPS, NV, D), 1.0, 6.0, ((0, 4), (1, 64)))
    query_time = draw_query_time(jax.random.fold_in(key_list[7], 71), 0)
    window = draw_window(jax.random.fold_in(key_list[7], 71), 0)
    return {"video_query": video_query, "audio_key": audio_key, "audio_value": audio_value, "out_weight": out_weight, "grad_out": grad_out, "query_time": query_time, "window": window}


def rotate(values, positions, sign):
    heads = values.shape[-1] // DH
    half = DH // 2
    shaped = values.astype(jnp.float32).reshape(values.shape[:-1] + (heads, DH))
    freqs = 10000.0 ** (-jnp.arange(half, dtype=jnp.float32) / half)
    angles = sign * positions.astype(jnp.float32)[:, None] * freqs[None, :]
    cosine = jnp.cos(angles)[:, None, :]
    sine = jnp.sin(angles)[:, None, :]
    first = shaped[..., :half]
    second = shaped[..., half:]
    turned = jnp.concatenate([first * cosine - second * sine, first * sine + second * cosine], axis=-1)
    return turned.reshape(values.shape)

def reference(video_query, audio_key, audio_value, out_weight, grad_out, query_time, window):
    heads = HD // DH
    scale = 1.0 / math.sqrt(DH)
    span = 3 * ATOK_DEV
    key_index = jnp.arange(NA, dtype=jnp.int32)
    query_rot = rotate(video_query, query_time, 1.0).astype(jnp.bfloat16)
    key_rot = rotate(audio_key, key_index, 1.0).astype(jnp.bfloat16)
    flat_grad = grad_out.reshape(CLIPS * NV, D)
    att_grad = jnp.dot(flat_grad, out_weight.T, preferred_element_type=jnp.float32)
    att_grad = att_grad.astype(jnp.bfloat16).reshape(CLIPS, NV, HD)

    def shard_step(carry, shard):
        key_total, value_total = carry
        first_row = (shard * VTOK_DEV).astype(jnp.int32)
        key_start = jnp.clip(shard * ATOK_DEV - ATOK_DEV, 0, NA - span).astype(jnp.int32)
        rows_query = lax.dynamic_slice_in_dim(query_rot, first_row, VTOK_DEV, 1).astype(jnp.float32)
        rows_grad = lax.dynamic_slice_in_dim(att_grad, first_row, VTOK_DEV, 1).astype(jnp.float32)
        near_keys = lax.dynamic_slice_in_dim(key_rot, key_start, span, 1).astype(jnp.float32)
        near_values = lax.dynamic_slice_in_dim(audio_value, key_start, span, 1).astype(jnp.float32)
        lower = lax.dynamic_slice_in_dim(window[0], first_row, VTOK_DEV, 0)
        upper = lax.dynamic_slice_in_dim(window[1], first_row, VTOK_DEV, 0)
        times = lax.dynamic_slice_in_dim(query_time, first_row, VTOK_DEV, 0)
        near_index = key_start + jnp.arange(span, dtype=jnp.int32)
        allowed = (near_index[:, None] >= lower[None, :]) & (near_index[:, None] < upper[None, :])
        query_heads = rows_query.reshape(CLIPS, VTOK_DEV, heads, DH)
        grad_heads = rows_grad.reshape(CLIPS, VTOK_DEV, heads, DH)
        key_heads = near_keys.reshape(CLIPS, span, heads, DH)
        value_heads = near_values.reshape(CLIPS, span, heads, DH)
        scores = scale * jnp.einsum('cqhd,ckhd->chkq', query_heads, key_heads)
        masked = jnp.where(allowed, scores, -1e+30)
        highest = lax.optimization_barrier(jnp.max(masked, axis=2, keepdims=True))
        expo = jnp.where(allowed, jnp.exp(masked - highest), 0.0)
        probs = expo / lax.optimization_barrier(jnp.sum(expo, axis=2, keepdims=True))
        probs_low = lax.optimization_barrier(probs.astype(jnp.bfloat16)).astype(jnp.float32)
        attended = jnp.einsum('chkq,ckhd->cqhd', probs_low, value_heads).astype(jnp.bfloat16)
        value_part = jnp.einsum('chkq,cqhd->ckhd', probs_low, grad_heads)
        prob_grad = jnp.einsum('cqhd,ckhd->chkq', grad_heads, value_heads)
        row_dot = lax.optimization_barrier(jnp.sum(probs * prob_grad, axis=2, keepdims=True))
        score_grad = probs * (prob_grad - row_dot)
        score_grad = lax.optimization_barrier(score_grad.astype(jnp.bfloat16)).astype(jnp.float32)
        query_part = scale * jnp.einsum('chkq,ckhd->cqhd', score_grad, key_heads)
        key_part = scale * jnp.einsum('chkq,cqhd->ckhd', score_grad, query_heads)
        query_grad = rotate(query_part.reshape(CLIPS, VTOK_DEV, HD), times, -1.0).astype(jnp.bfloat16)
        old_keys = lax.dynamic_slice_in_dim(key_total, key_start, span, 1)
        key_total = lax.dynamic_update_slice_in_dim(key_total, old_keys + key_part.reshape(CLIPS, span, HD), key_start, 1)
        old_values = lax.dynamic_slice_in_dim(value_total, key_start, span, 1)
        value_total = lax.dynamic_update_slice_in_dim(value_total, old_values + value_part.reshape(CLIPS, span, HD), key_start, 1)
        return ((key_total, value_total), (attended.reshape(CLIPS, VTOK_DEV, HD), query_grad))
    start_totals = (jnp.zeros((CLIPS, NA, HD), jnp.float32), jnp.zeros((CLIPS, NA, HD), jnp.float32))
    (key_total, value_total), (attended_all, query_all) = lax.scan(shard_step, start_totals, jnp.arange(N_CTX, dtype=jnp.int32))
    attended_all = jnp.transpose(attended_all, (1, 0, 2, 3)).reshape(CLIPS * NV, HD)
    query_grad = jnp.transpose(query_all, (1, 0, 2, 3)).reshape(CLIPS, NV, HD)
    output = jnp.dot(attended_all, out_weight, preferred_element_type=jnp.float32).astype(jnp.bfloat16).reshape(CLIPS, NV, D)
    factor = 1.0 / math.sqrt(CLIPS * NV)
    weight_grad = factor * jnp.dot(attended_all.T, flat_grad, preferred_element_type=jnp.float32)
    key_grad = rotate(key_total, key_index, -1.0)
    return (output, query_grad, key_grad, value_total, weight_grad)
```

```python
import math

import jax
import jax.numpy as jnp
import numpy as np
from jax import lax
from jax.experimental import pallas as pl
from jax.experimental.pallas import tpu as pltpu
from jax.sharding import PartitionSpec as P

DH = 64
HALF = DH // 2
TOK = 512
WIDTH = 1024
SPAN = 8
NEAR = 3 * SPAN
GROUPS = 4
GW = WIDTH // GROUPS
GH = GW // DH
SCALE = 1.0 / math.sqrt(DH)
MESH = pl.DeviceIdType.MESH
BF = jnp.bfloat16
F32 = jnp.float32

NN = (((1,), (0,)), ((), ()))
NT = (((1,), (1,)), ((), ()))
TN = (((0,), (0,)), ((), ()))


def dot(a, b, dims):
    return lax.dot_general(a, b, dims, preferred_element_type=F32)


def flip(value, mask, bits):
    out = 0
    for bit in range(bits):
        digit = (value // (1 << bit)) % 2
        if (mask >> bit) & 1:
            digit = 1 - digit
        out = out + digit * (1 << bit)
    return out


def kernel(
    factor,
    query_hbm,
    key_ref,
    value_ref,
    weight_hbm,
    grad_hbm,
    cos_ref,
    sin_ref,
    window_ref,
    out_hbm,
    qgrad_hbm,
    kgrad_ref,
    vgrad_ref,
    wgrad_ref,
    q_raw,
    q_rot,
    near_kv,
    w_all,
    g_own,
    g_pair,
    probs_s,
    att,
    att_t,
    att_t_pair,
    ag32,
    ag,
    qg,
    kp,
    vp,
    halo_out,
    halo_in,
    out_stage,
    s1,
    r1,
    s2,
    r2,
    t1,
    p1,
    t2,
    p2,
    u,
    v,
    loc,
    sem_s,
    sem_r,
):
    ctx = lax.axis_index("ctx")
    fs = lax.axis_index("fsdp")
    z = ctx // 8
    y = (ctx // 2) % 4
    xl = ctx % 2
    xh = fs // 2
    core = fs % 2
    x = xh * 2 + xl
    n_ctx = 64

    def device(x_, y_, z_, core_):
        return (z_ * 8 + y_ * 2 + x_ % 2, (x_ // 2) * 2 + core_)

    pair = (ctx, xh * 2 + 1 - core)
    after = ((ctx + 1) % n_ctx, fs)
    before = ((ctx + n_ctx - 1) % n_ctx, fs)
    x_peer = [device(flip(x, m, 2), y, z, core) for m in (1, 2, 3)]
    y_peer = [device(x, flip(y, m, 2), z, core) for m in (1, 2, 3)]
    z_peer = [device(x, y, flip(z, m, 3), core) for m in range(1, 8)]
    z_step = {d: device(x, y, (z + d + 8) % 8, core) for d in (1, -1, 2, -2)}

    counter = [0]

    def remote(src, dst, target):
        index = counter[0]
        counter[0] += 1
        copy = pltpu.make_async_remote_copy(
            src_ref=src,
            dst_ref=dst,
            send_sem=sem_s.at[index],
            recv_sem=sem_r.at[index],
            device_id=target,
            device_id_type=MESH,
        )
        copy.start()
        started.append(copy)
        return copy

    started = []
    local_counter = [0]

    def local(src, dst):
        index = local_counter[0]
        local_counter[0] += 1
        copy = pltpu.make_async_copy(src, dst, loc.at[index])
        copy.start()
        return copy

    block = fs
    pair_block = xh * 2 + 1 - core
    far_block = (1 - xh) * 2 + core
    far_pair_block = (1 - xh) * 2 + 1 - core
    load_q = [local(query_hbm.at[:, pl.ds(i * GW, GW)], q_raw.at[i]) for i in range(GROUPS)]
    load_g = [local(grad_hbm.at[:, pl.ds(i * WIDTH, WIDTH)], g_own.at[i]) for i in range(4)]
    load_w = local(weight_hbm, w_all.at[block])

    barrier = pltpu.get_barrier_semaphore()
    greet = [pair, after, before] + x_peer + y_peer + z_peer
    for target in greet:
        pl.semaphore_signal(barrier, inc=1, device_id=target, device_id_type=MESH)

    lane_i = lax.broadcasted_iota(jnp.int32, (GW, GW), 0)
    lane_j = lax.broadcasted_iota(jnp.int32, (GW, GW), 1)
    first_j = lane_j % DH < HALF
    turn = jnp.where(
        first_j & (lane_i == lane_j + HALF),
        -1.0,
        jnp.where((~first_j) & (lane_i == lane_j - HALF), 1.0, 0.0),
    ).astype(BF)
    cos_k = jnp.concatenate([cos_ref[pl.ds(TOK, SPAN), :]] * 2, axis=1)
    sin_k = jnp.concatenate([sin_ref[pl.ds(TOK, SPAN), :]] * 2, axis=1)
    for i in range(GROUPS):
        sl = slice(i * GW, (i + 1) * GW)
        raw = key_ref[:, sl]
        turned = raw.astype(F32) * cos_k + dot(raw, turn, NN) * sin_k
        near_kv[0, :, sl] = jnp.concatenate([turned, value_ref[:, sl].astype(F32)], axis=0).astype(BF)

    pl.semaphore_wait(barrier, len(greet))

    halo_a = remote(near_kv.at[0], near_kv.at[1], after)
    halo_b = remote(near_kv.at[0], near_kv.at[2], before)
    quarter = z % 4
    cross = []
    for half in range(2):
        rows = pl.ds(quarter * 256 + half * 128, 128)
        cross.append(remote(weight_hbm.at[rows], w_all.at[block, rows], x_peer[2]))
    pair_g = [
        remote(
            grad_hbm.at[:, pl.ds(pl.multiple_of((2 * h + 1 - core) * WIDTH, WIDTH), WIDTH)],
            g_pair.at[h],
            pair,
        )
        for h in range(2)
    ]
    pair_w = remote(weight_hbm, w_all.at[block], pair)

    cos_q = jnp.concatenate([cos_ref[pl.ds(0, TOK), :]] * 2, axis=1)
    sin_q = jnp.concatenate([sin_ref[pl.ds(0, TOK), :]] * 2, axis=1)
    for copy in load_q:
        copy.wait()

    @pl.loop(0, GROUPS)
    def _(i):
        raw = q_raw[i]
        q_rot[i] = (raw.astype(F32) * cos_q + dot(raw, turn, NN) * sin_q).astype(BF)

    halo_a.wait_recv()
    halo_b.wait_recv()

    near_index = (
        lax.broadcasted_iota(jnp.int32, (NEAR, TOK), 0) + ctx * SPAN - SPAN
    )
    allowed = (near_index >= window_ref[0:1, :]) & (near_index < window_ref[1:2, :])
    head_row = lax.broadcasted_iota(jnp.int32, (GH, NEAR, GW), 0)
    head_col = lax.broadcasted_iota(jnp.int32, (GH, NEAR, GW), 2) // DH
    own_head = head_row == head_col

    def spread(row, i):
        sl = pl.ds(pl.multiple_of(i * GW, GW), GW)
        parts = [near_kv[slot, :, sl].astype(F32)[row : row + SPAN] for slot in (1, 0, 2)]
        near = jnp.concatenate(parts, axis=0)
        wide = jnp.where(own_head, near[None], 0.0)
        return wide.reshape(GH * NEAR, GW).astype(BF)

    def gather_heads(wide):
        shaped = wide.reshape(GH, NEAR, GW)
        return jnp.sum(jnp.where(own_head, shaped, 0.0), axis=0)

    @pl.loop(0, GROUPS)
    def _(i):
        keys = spread(0, i)
        values = spread(SPAN, i)
        scores = SCALE * dot(keys, q_rot[i], NT).reshape(GH, NEAR, TOK)
        masked = jnp.where(allowed[None], scores, -1e30)
        highest = jnp.max(masked, axis=1, keepdims=True)
        expo = jnp.where(allowed[None], jnp.exp(masked - highest), 0.0)
        probs = (expo / jnp.sum(expo, axis=1, keepdims=True)).reshape(GH * NEAR, TOK)
        probs_s[i] = probs
        low = probs.astype(BF)
        att[i] = dot(low, values, TN).astype(BF)
        att_t[pl.ds(pl.multiple_of(i * GW, GW), GW), :] = dot(values, low, TN).astype(BF)

    pair_a = remote(att_t, att_t_pair, pair)

    far_moves = []

    def pass_on(half):
        cross[half].wait_recv()
        rows = pl.ds(quarter * 256 + half * 128, 128)
        piece = w_all.at[far_block, rows]
        moves = [
            remote(piece, piece, z_step[1]),
            remote(piece, piece, z_step[-1]),
            remote(piece, piece, z_step[2 if half == 0 else -2]),
            remote(piece, piece, pair),
        ]
        far_moves.append(moves)

    pass_on(0)

    for copy in load_g:
        copy.wait()
    for copy in pair_g:
        copy.wait_recv()
    pair_a.wait_recv()

    def gradient(h, part, store):
        cols = slice(part * 512, (part + 1) * 512)

        @pl.loop(0, 2)
        def _(i):
            rows = pl.ds(pl.multiple_of(i * 512, 512), 512)
            total = dot(att_t[rows, :], g_own[2 * h + core, :, cols], NN)
            total = total + dot(att_t_pair[rows, :], g_pair[h, :, cols], NN)
            store(i, total.astype(BF).reshape(4, 4, 2, 16, 512))

    def store_x(h):
        def store(i, total):
            for low_x in range(2):
                s1[2 * h + low_x, pl.ds(i * 4, 4)] = total[:, :, low_x]

        return store

    def store_y(h):
        def store(i, total):
            for to_y in range(4):
                s2[to_y, h, pl.ds(i * 4, 4)] = total[:, to_y]

        return store

    x_moves = {}

    def send_x(m):
        x_moves[m] = remote(s1.at[flip(x, m, 2)], r1.at[m - 1], x_peer[m - 1])

    y_moves = {}

    def send_y(m, h):
        y_moves[m, h] = remote(s2.at[flip(y, m, 2), h], r2.at[m - 1, h], y_peer[m - 1])

    gradient(1 - xh, 0, store_x(1 - xh))
    send_x(2)
    send_x(3)
    gradient(0, 1, store_y(0))
    for m in (1, 2, 3):
        send_y(m, 0)
    gradient(xh, 0, store_x(xh))
    send_x(1)
    pass_on(1)
    gradient(1, 1, store_y(1))
    for m in (1, 2, 3):
        send_y(m, 1)

    load_w.wait()
    pair_w.wait_recv()

    out_moves = []

    def project(b):
        @pl.loop(0, 2)
        def _(j):
            cols = pl.ds(pl.multiple_of(j * 512, 512), 512)
            total = dot(att[0], w_all[b, 0:GW, cols], NN)
            for i in range(1, GROUPS):
                total = total + dot(att[i], w_all[b, i * GW : (i + 1) * GW, cols], NN)
            out_stage[b, :, cols] = total.astype(BF)

        out_moves.append(
            local(out_stage.at[b], out_hbm.at[:, pl.ds(pl.multiple_of(b * WIDTH, WIDTH), WIDTH)])
        )

    @pl.loop(0, 2)
    def _(j):
        rows = pl.ds(pl.multiple_of(j * 512, 512), 512)
        ag32[j] = dot(g_own[block], w_all[block, rows, :], NT) + dot(
            g_own[pair_block], w_all[pair_block, rows, :], NT
        )

    project(block)
    project(pair_block)

    for half in range(2):
        rows = [
            pl.ds(((z + 3) % 4) * 256 + half * 128, 128),
            pl.ds(((z + 1) % 4) * 256 + half * 128, 128),
            pl.ds(((z + 2) % 4) * 256 + half * 128, 128),
        ]
        for k in range(3):
            far_moves[half][k].wait_recv()
            piece = w_all.at[far_block, rows[k]]
            far_moves[half].append(remote(piece, piece, pair))

    for m in (1, 2, 3):
        x_moves[m].wait_recv()

    @pl.loop(0, 4)
    def _(to_y):
        total = s1[x, :, to_y].astype(F32)
        for m in range(3):
            total = total + r1[m, :, to_y].astype(F32)
        t1[to_y] = total.astype(BF)

    y2_moves = [remote(t1.at[flip(y, m, 2)], p1.at[m - 1], y_peer[m - 1]) for m in (1, 2, 3)]
    for m in (1, 2, 3):
        for h in range(2):
            y_moves[m, h].wait_recv()

    @pl.loop(0, 4)
    def _(to_x):
        h = to_x // 2
        low_x = to_x % 2
        total = s2[y, h, :, low_x].astype(F32)
        for m in range(3):
            total = total + r2[m, h, :, low_x].astype(F32)
        t2[to_x] = total.astype(BF)

    x2_moves = [remote(t2.at[flip(x, m, 2)], p2.at[m - 1], x_peer[m - 1]) for m in (1, 2, 3)]

    for half in range(2):
        for k in range(3, 7):
            far_moves[half][k].wait_recv()

    @pl.loop(0, 2)
    def _(j):
        rows = pl.ds(pl.multiple_of(j * 512, 512), 512)
        total = ag32[j] + dot(g_own[far_block], w_all[far_block, rows, :], NT)
        total = total + dot(g_own[far_pair_block], w_all[far_pair_block, rows, :], NT)
        low = total.astype(BF)
        ag[2 * j] = low[:, :GW]
        ag[2 * j + 1] = low[:, GW:]

    @pl.loop(0, GROUPS)
    def _(i):
        keys = spread(0, i)
        values = spread(SPAN, i)
        grads = ag[i]
        probs = probs_s[i]
        low = probs.astype(BF)
        sl = pl.ds(pl.multiple_of(i * GW, GW), GW)
        vp[:, sl] = gather_heads(dot(low, grads, NN))
        shaped = probs.reshape(GH, NEAR, TOK)
        prob_grad = dot(values, grads, NT).reshape(GH, NEAR, TOK)
        row_dot = jnp.sum(shaped * prob_grad, axis=1, keepdims=True)
        score_grad = (shaped * (prob_grad - row_dot)).reshape(GH * NEAR, TOK).astype(BF)
        turned_keys = dot(keys, turn, NN).astype(BF)
        part = SCALE * dot(score_grad, keys, TN)
        part_turned = SCALE * dot(score_grad, turned_keys, TN)
        qg[i] = (part * cos_q - part_turned * sin_q).astype(BF)
        kp[:, sl] = gather_heads(SCALE * dot(score_grad, q_rot[i], NN))

    halo_out[0, 0:SPAN] = kp[2 * SPAN :, :]
    halo_out[0, SPAN:] = vp[2 * SPAN :, :]
    halo_out[1, 0:SPAN] = kp[0:SPAN, :]
    halo_out[1, SPAN:] = vp[0:SPAN, :]
    back = [
        remote(halo_out.at[0], halo_in.at[0], after),
        remote(halo_out.at[1], halo_in.at[1], before),
    ]
    for i in range(GROUPS):
        out_moves.append(local(qg.at[i], qgrad_hbm.at[:, pl.ds(i * GW, GW)]))

    project(far_block)

    for copy in y2_moves + x2_moves:
        copy.wait_recv()
    first = t1[y].astype(F32)
    second = t2[x].astype(F32)
    for m in range(3):
        first = first + p1[m].astype(F32)
        second = second + p2[m].astype(F32)
    u[:, :, 0:512] = first.astype(BF)
    u[:, :, 512:1024] = second.astype(BF)
    z_moves = [remote(u.at[flip(z, m, 3)], v.at[m - 1], z_peer[m - 1]) for m in range(1, 8)]

    project(far_pair_block)

    for copy in back:
        copy.wait_recv()
    vgrad_ref[...] = vp[SPAN : 2 * SPAN, :] + halo_in[0, SPAN:] + halo_in[1, SPAN:]
    key_total = kp[SPAN : 2 * SPAN, :] + halo_in[0, 0:SPAN] + halo_in[1, 0:SPAN]
    lane = lax.broadcasted_iota(jnp.int32, (SPAN, WIDTH), 1) % DH
    other = jnp.where(
        lane < HALF,
        -pltpu.roll(key_total, WIDTH - HALF, 1),
        pltpu.roll(key_total, HALF, 1),
    )
    wide_cos = jnp.concatenate([cos_k] * GROUPS, axis=1)
    wide_sin = jnp.concatenate([sin_k] * GROUPS, axis=1)
    kgrad_ref[...] = key_total * wide_cos - other * wide_sin

    for copy in z_moves:
        copy.wait_recv()
    total = u[z].astype(F32)
    for m in range(7):
        total = total + v[m].astype(F32)
    wgrad_ref[...] = total * factor

    for copy in out_moves:
        copy.wait()
    for copy in started:
        copy.wait_send()


def local(video_query, audio_key, audio_value, out_weight, grad_out, query_time, window):
    shard = lax.axis_index("ctx")
    freqs = np.tile((10000.0 ** (-np.arange(HALF) / HALF)).astype(np.float32), 128 // HALF)
    key_index = shard * SPAN + jnp.arange(SPAN, dtype=jnp.int32)
    positions = jnp.concatenate([query_time, key_index]).astype(F32)
    angles = positions[:, None] * freqs[None, :]
    factor = 1.0 / math.sqrt(TOK * lax.axis_size("ctx") * lax.axis_size("fsdp"))

    vmem = pl.BlockSpec(memory_space=pltpu.VMEM)
    hbm = pl.BlockSpec(memory_space=pl.ANY)
    n_sems = 48

    def body(*refs):
        kernel(factor, *refs)

    outs = pl.pallas_call(
        body,
        name="fused",
        out_shape=(
            jax.ShapeDtypeStruct((TOK, 4 * WIDTH), BF),
            jax.ShapeDtypeStruct((TOK, WIDTH), BF),
            jax.ShapeDtypeStruct((SPAN, WIDTH), F32),
            jax.ShapeDtypeStruct((SPAN, WIDTH), F32),
            jax.ShapeDtypeStruct((16, WIDTH), F32),
        ),
        in_specs=[hbm, vmem, vmem, hbm, hbm, vmem, vmem, vmem],
        out_specs=(hbm, hbm, vmem, vmem, vmem),
        scratch_shapes=[
            pltpu.VMEM((GROUPS, TOK, GW), BF),
            pltpu.VMEM((GROUPS, TOK, GW), BF),
            pltpu.VMEM((3, 2 * SPAN, WIDTH), BF),
            pltpu.VMEM((4, WIDTH, WIDTH), BF),
            pltpu.VMEM((4, TOK, WIDTH), BF),
            pltpu.VMEM((2, TOK, WIDTH), BF),
            pltpu.VMEM((GROUPS, GH * NEAR, TOK), F32),
            pltpu.VMEM((GROUPS, TOK, GW), BF),
            pltpu.VMEM((WIDTH, TOK), BF),
            pltpu.VMEM((WIDTH, TOK), BF),
            pltpu.VMEM((2, TOK, 512), F32),
            pltpu.VMEM((GROUPS, TOK, GW), BF),
            pltpu.VMEM((GROUPS, TOK, GW), BF),
            pltpu.VMEM((NEAR, WIDTH), F32),
            pltpu.VMEM((NEAR, WIDTH), F32),
            pltpu.VMEM((2, 2 * SPAN, WIDTH), F32),
            pltpu.VMEM((2, 2 * SPAN, WIDTH), F32),
            pltpu.VMEM((4, TOK, WIDTH), BF),
            pltpu.VMEM((4, 8, 4, 16, 512), BF),
            pltpu.VMEM((3, 8, 4, 16, 512), BF),
            pltpu.VMEM((4, 2, 8, 2, 16, 512), BF),
            pltpu.VMEM((3, 2, 8, 2, 16, 512), BF),
            pltpu.VMEM((4, 8, 16, 512), BF),
            pltpu.VMEM((3, 8, 16, 512), BF),
            pltpu.VMEM((4, 8, 16, 512), BF),
            pltpu.VMEM((3, 8, 16, 512), BF),
            pltpu.VMEM((8, 16, WIDTH), BF),
            pltpu.VMEM((7, 16, WIDTH), BF),
            pltpu.SemaphoreType.DMA((24,)),
            pltpu.SemaphoreType.DMA((n_sems,)),
            pltpu.SemaphoreType.DMA((n_sems,)),
        ],
        compiler_params=pltpu.CompilerParams(
            collective_id=0, has_side_effects=True, vmem_limit_bytes=58 << 20
        ),
    )(
        video_query[0],
        audio_key[0],
        audio_value[0],
        out_weight,
        grad_out[0],
        jnp.cos(angles),
        jnp.sin(angles),
        window,
    )
    output, query_grad, key_grad, value_grad, weight_grad = outs
    return (output[None], query_grad[None], key_grad[None], value_grad[None], weight_grad)


def solution(mesh):
    in_specs = (
        P("fsdp", "ctx", None),
        P("fsdp", "ctx", None),
        P("fsdp", "ctx", None),
        P(None, "fsdp"),
        P("fsdp", "ctx", None),
        P("ctx"),
        P(None, "ctx"),
    )
    out_specs = (
        P("fsdp", "ctx", None),
        P("fsdp", "ctx", None),
        P("fsdp", "ctx", None),
        P("fsdp", "ctx", None),
        P("ctx", "fsdp"),
    )
    return jax.shard_map(local, mesh=mesh, in_specs=in_specs, out_specs=out_specs, check_vma=False)
```

```python
import math

import jax
import jax.numpy as jnp
import numpy as np
from jax import lax
from jax.experimental import pallas as pl
from jax.experimental.pallas import tpu as pltpu
from jax.sharding import PartitionSpec as P

DH = 64
HALF = DH // 2
TOK = 512
WIDTH = 1024
SPAN = 8
NEAR = 3 * SPAN
GROUPS = 4
GW = WIDTH // GROUPS
GH = GW // DH
SCALE = 1.0 / math.sqrt(DH)
MESH = pl.DeviceIdType.MESH
BF = jnp.bfloat16
F32 = jnp.float32

NN = (((1,), (0,)), ((), ()))
NT = (((1,), (1,)), ((), ()))
TN = (((0,), (0,)), ((), ()))


def dot(a, b, dims):
    return lax.dot_general(a, b, dims, preferred_element_type=F32)


def flip(value, mask, bits):
    out = 0
    for bit in range(bits):
        digit = (value // (1 << bit)) % 2
        if (mask >> bit) & 1:
            digit = 1 - digit
        out = out + digit * (1 << bit)
    return out


def kernel(
    factor,
    query_hbm,
    key_ref,
    value_ref,
    weight_hbm,
    grad_hbm,
    time_ref,
    window_ref,
    freq_ref,
    out_stage,
    qgrad,
    kgrad_ref,
    vgrad_ref,
    wgrad_ref,
    q_raw,
    q_rot,
    near_kv,
    w_all,
    g_own,
    g_pair,
    probs_s,
    att,
    att_t,
    att_t_pair,
    ag32,
    ag,
    table,
    kp,
    vp,
    halo_out,
    halo_in,
    s1,
    r1,
    s2,
    r2,
    t1,
    p1,
    t2,
    p2,
    u,
    v,
    loc,
    sem_s,
    sem_r,
):
    ctx = lax.axis_index("ctx")
    fs = lax.axis_index("fsdp")
    z = ctx // 8
    y = (ctx // 2) % 4
    xl = ctx % 2
    xh = fs // 2
    core = fs % 2
    x = xh * 2 + xl
    n_ctx = 64

    def device(x_, y_, z_, core_):
        return (z_ * 8 + y_ * 2 + x_ % 2, (x_ // 2) * 2 + core_)

    pair = (ctx, xh * 2 + 1 - core)
    after = ((ctx + 1) % n_ctx, fs)
    before = ((ctx + n_ctx - 1) % n_ctx, fs)
    x_peer = [device(flip(x, m, 2), y, z, core) for m in (1, 2, 3)]
    y_peer = [device(x, flip(y, m, 2), z, core) for m in (1, 2, 3)]
    z_peer = [device(x, y, flip(z, m, 3), core) for m in range(1, 8)]
    z_step = {d: device(x, y, (z + d + 8) % 8, core) for d in (1, -1, 2, -2)}

    counter = [0]

    def remote(src, dst, target):
        index = counter[0]
        counter[0] += 1
        copy = pltpu.make_async_remote_copy(
            src_ref=src,
            dst_ref=dst,
            send_sem=sem_s.at[index],
            recv_sem=sem_r.at[index],
            device_id=target,
            device_id_type=MESH,
        )
        copy.start()
        started.append(copy)
        return copy

    started = []
    local_counter = [0]

    def local(src, dst):
        index = local_counter[0]
        local_counter[0] += 1
        copy = pltpu.make_async_copy(src, dst, loc.at[index])
        copy.start()
        return copy

    block = fs
    pair_block = xh * 2 + 1 - core
    far_block = (1 - xh) * 2 + core
    far_pair_block = (1 - xh) * 2 + 1 - core
    load_q = [local(query_hbm.at[:, pl.ds(i * GW, GW)], q_raw.at[i]) for i in range(GROUPS)]
    load_g = [local(grad_hbm.at[:, pl.ds(i * WIDTH, WIDTH)], g_own.at[i]) for i in range(4)]
    load_w = local(weight_hbm, w_all.at[block])

    barrier = pltpu.get_barrier_semaphore()
    greet = [pair, after, before] + x_peer + y_peer + z_peer
    for target in greet:
        pl.semaphore_signal(barrier, inc=1, device_id=target, device_id_type=MESH)

    lane_i = lax.broadcasted_iota(jnp.int32, (GW, GW), 0)
    lane_j = lax.broadcasted_iota(jnp.int32, (GW, GW), 1)
    first_j = lane_j % DH < HALF
    turn = jnp.where(
        first_j & (lane_i == lane_j + HALF),
        -1.0,
        jnp.where((~first_j) & (lane_i == lane_j - HALF), 1.0, 0.0),
    ).astype(BF)
    near_row = lax.broadcasted_iota(jnp.int32, (32, 1), 0) + ctx * SPAN - SPAN
    angles = near_row.astype(F32) * freq_ref[...]
    near_table = jnp.concatenate([jnp.cos(angles), jnp.sin(angles)], axis=1)
    pieces = []
    rest = near_table
    for _ in range(3):
        piece = rest.astype(BF).astype(F32)
        pieces.append(piece)
        rest = rest - piece
    time_row = jnp.where(near_row == time_ref[...], 1.0, 0.0)
    chosen = jnp.concatenate([time_row] * 3, axis=0).astype(BF)
    table[...] = dot(chosen, jnp.concatenate(pieces, axis=0).astype(BF), TN)

    def cos_q():
        return jnp.concatenate([table[:, :128]] * 2, axis=1)

    def sin_q():
        return jnp.concatenate([table[:, 128:]] * 2, axis=1)

    cos_k = jnp.concatenate([near_table[SPAN : 2 * SPAN, :128]] * 2, axis=1)
    sin_k = jnp.concatenate([near_table[SPAN : 2 * SPAN, 128:]] * 2, axis=1)
    for i in range(GROUPS):
        sl = slice(i * GW, (i + 1) * GW)
        raw = key_ref[:, sl]
        turned = raw.astype(F32) * cos_k + dot(raw, turn, NN) * sin_k
        near_kv[0, :, sl] = jnp.concatenate([turned, value_ref[:, sl].astype(F32)], axis=0).astype(BF)

    pl.semaphore_wait(barrier, len(greet))

    halo_a = remote(near_kv.at[0], near_kv.at[1], after)
    halo_b = remote(near_kv.at[0], near_kv.at[2], before)
    quarter = z % 4
    cross = []
    for half in range(2):
        rows = pl.ds(quarter * 256 + half * 128, 128)
        cross.append(remote(weight_hbm.at[rows], w_all.at[block, rows], x_peer[2]))
    pair_g = [
        remote(
            grad_hbm.at[:, pl.ds(pl.multiple_of((2 * h + 1 - core) * WIDTH, WIDTH), WIDTH)],
            g_pair.at[h],
            pair,
        )
        for h in range(2)
    ]

    for copy in load_q:
        copy.wait()

    @pl.loop(0, GROUPS)
    def _(i):
        raw = q_raw[i]
        q_rot[i] = (raw.astype(F32) * cos_q() + dot(raw, turn, NN) * sin_q()).astype(BF)

    def early(j):
        rows = pl.ds(j * 512, 512)
        ag32[j] = dot(g_own[block], w_all[block, rows, :], NT)

    for copy in load_g:
        copy.wait()
    load_w.wait()
    early(0)

    halo_a.wait_recv()
    halo_b.wait_recv()

    near_index = (
        lax.broadcasted_iota(jnp.int32, (NEAR, TOK), 0) + ctx * SPAN - SPAN
    )
    allowed = (near_index >= window_ref[0:1, :]) & (near_index < window_ref[1:2, :])
    head_row = lax.broadcasted_iota(jnp.int32, (GH, NEAR, GW), 0)
    head_col = lax.broadcasted_iota(jnp.int32, (GH, NEAR, GW), 2) // DH
    own_head = head_row == head_col

    def spread(row, i):
        sl = pl.ds(pl.multiple_of(i * GW, GW), GW)
        parts = [near_kv[slot, :, sl].astype(F32)[row : row + SPAN] for slot in (1, 0, 2)]
        near = jnp.concatenate(parts, axis=0)
        wide = jnp.where(own_head, near[None], 0.0)
        return wide.reshape(GH * NEAR, GW).astype(BF)

    def gather_heads(wide):
        shaped = wide.reshape(GH, NEAR, GW)
        return jnp.sum(jnp.where(own_head, shaped, 0.0), axis=0)

    pair_a = []
    for i in range(GROUPS):
        keys = spread(0, i)
        values = spread(SPAN, i)
        scores = SCALE * dot(keys, q_rot[i], NT).reshape(GH, NEAR, TOK)
        masked = jnp.where(allowed[None], scores, -1e30)
        highest = jnp.max(masked, axis=1, keepdims=True)
        expo = jnp.where(allowed[None], jnp.exp(masked - highest), 0.0)
        probs = (expo / jnp.sum(expo, axis=1, keepdims=True)).reshape(GH * NEAR, TOK)
        probs_s[i] = probs
        low = probs.astype(BF)
        rows = pl.ds(i * GW, GW)
        att_t[rows, :] = dot(values, low, TN).astype(BF)
        pair_a.append(remote(att_t.at[rows], att_t_pair.at[rows], pair))
        att[i] = dot(low, values, TN).astype(BF)

    pair_w = remote(weight_hbm, w_all.at[block], pair)
    early(1)

    far_moves = []

    def pass_on(half):
        cross[half].wait_recv()
        rows = pl.ds(quarter * 256 + half * 128, 128)
        piece = w_all.at[far_block, rows]
        moves = [
            remote(piece, piece, z_step[1]),
            remote(piece, piece, z_step[-1]),
            remote(piece, piece, z_step[2 if half == 0 else -2]),
            remote(piece, piece, pair),
        ]
        far_moves.append(moves)

    for copy in pair_g + pair_a:
        copy.wait_recv()

    def gradient(h, part, store):
        cols = slice(part * 512, (part + 1) * 512)

        @pl.loop(0, 2)
        def _(i):
            rows = pl.ds(pl.multiple_of(i * 512, 512), 512)
            total = dot(att_t[rows, :], g_own[2 * h + core, :, cols], NN)
            total = total + dot(att_t_pair[rows, :], g_pair[h, :, cols], NN)
            store(i, total.astype(BF).reshape(4, 4, 2, 16, 512))

    def store_x(h):
        def store(i, total):
            for low_x in range(2):
                for k in range(2):
                    s1[2 * h + low_x, k, pl.ds(i * 4, 4)] = total[:, :, low_x, :, k * 256 : k * 256 + 256]

        return store

    def store_y(h):
        def store(i, total):
            for to_y in range(4):
                for k in range(2):
                    s2[to_y, k, h, pl.ds(i * 4, 4)] = total[:, to_y, :, :, k * 256 : k * 256 + 256]

        return store

    near = (1, 3)
    x_first = {}
    y_first = {}

    def send_x(k, slot):
        to = flip(x, 2 if slot == 0 else near[k], 2)
        x_first[k, slot] = remote(s1.at[to, k], r1.at[k, slot], x_peer[near[k] - 1])

    def send_y(k, slot, h):
        to = flip(y, 2 if slot == 0 else near[k], 2)
        y_first[k, slot, h] = remote(s2.at[to, k, h], r2.at[k, slot, h], y_peer[near[k] - 1])

    gradient(1 - xh, 0, store_x(1 - xh))
    send_x(1, 0)
    send_x(0, 0)
    send_x(1, 1)
    pass_on(0)
    for h in range(2):
        gradient(h, 1, store_y(h))
        for slot in range(2):
            for k in range(2):
                send_y(k, slot, h)
    gradient(xh, 0, store_x(xh))
    send_x(0, 1)
    pass_on(1)

    x_second = []
    y_second = []
    for k in range(2):
        to = flip(x, near[1 - k], 2)
        x_first[k, 0].wait_recv()

        @pl.loop(0, 4)
        def _(i):
            part = pl.ds(i * 2, 2)
            s1[to, k, part] = (s1[to, k, part].astype(F32) + r1[k, 0, part].astype(F32)).astype(BF)

        x_second.append(remote(s1.at[to, k], r1.at[k, 2], x_peer[near[1 - k] - 1]))
    for k in range(2):
        to = flip(y, near[1 - k], 2)
        for h in range(2):
            y_first[k, 0, h].wait_recv()

            @pl.loop(0, 2)
            def _(i):
                part = pl.ds(i * 4, 4)
                s2[to, k, h, part] = (
                    s2[to, k, h, part].astype(F32) + r2[k, 0, h, part].astype(F32)
                ).astype(BF)

        y_second.append(remote(s2.at[to, k], r2.at[k, 2], y_peer[near[1 - k] - 1]))

    pair_w.wait_recv()

    def project(b):
        @pl.loop(0, 2)
        def _(j):
            cols = pl.ds(pl.multiple_of(j * 512, 512), 512)
            out_cols = pl.ds(pl.multiple_of(b * WIDTH + j * 512, 512), 512)
            total = dot(att[0], w_all[b, 0:GW, cols], NN)
            for i in range(1, GROUPS):
                total = total + dot(att[i], w_all[b, i * GW : (i + 1) * GW, cols], NN)
            out_stage[:, out_cols] = total.astype(BF)

    @pl.loop(0, 2)
    def _(j):
        rows = pl.ds(pl.multiple_of(j * 512, 512), 512)
        ag32[j] += dot(g_own[pair_block], w_all[pair_block, rows, :], NT)

    project(block)
    project(pair_block)

    for half in range(2):
        rows = [
            pl.ds(((z + 3) % 4) * 256 + half * 128, 128),
            pl.ds(((z + 1) % 4) * 256 + half * 128, 128),
            pl.ds(((z + 2) % 4) * 256 + half * 128, 128),
        ]
        for k in range(3):
            far_moves[half][k].wait_recv()
            piece = w_all.at[far_block, rows[k]]
            far_moves[half].append(remote(piece, piece, pair))

    for k in range(2):
        x_first[k, 1].wait_recv()
        x_second[k].wait_recv()

    @pl.loop(0, 4)
    def _(to_y):
        for k in range(2):
            total = s1[x, k, :, to_y].astype(F32)
            for m in (1, 2):
                total = total + r1[k, m, :, to_y].astype(F32)
            t1[to_y, :, :, k * 256 : k * 256 + 256] = total.astype(BF)

    y2_moves = [remote(t1.at[flip(y, m, 2)], p1.at[m - 1], y_peer[m - 1]) for m in (1, 2, 3)]
    for k in range(2):
        for h in range(2):
            y_first[k, 1, h].wait_recv()
        y_second[k].wait_recv()

    @pl.loop(0, 4)
    def _(to_x):
        h = to_x // 2
        low_x = to_x % 2
        for k in range(2):
            total = s2[y, k, h, :, low_x].astype(F32)
            for m in (1, 2):
                total = total + r2[k, m, h, :, low_x].astype(F32)
            t2[to_x, :, :, k * 256 : k * 256 + 256] = total.astype(BF)

    x2_moves = [remote(t2.at[flip(x, m, 2)], p2.at[m - 1], x_peer[m - 1]) for m in (1, 2, 3)]

    for half in range(2):
        for k in range(3, 7):
            far_moves[half][k].wait_recv()

    @pl.loop(0, 2)
    def _(j):
        rows = pl.ds(pl.multiple_of(j * 512, 512), 512)
        total = ag32[j] + dot(g_own[far_block], w_all[far_block, rows, :], NT)
        total = total + dot(g_own[far_pair_block], w_all[far_pair_block, rows, :], NT)
        low = total.astype(BF)
        ag[2 * j] = low[:, :GW]
        ag[2 * j + 1] = low[:, GW:]

    @pl.loop(0, GROUPS)
    def _(i):
        keys = spread(0, i)
        values = spread(SPAN, i)
        grads = ag[i]
        probs = probs_s[i]
        low = probs.astype(BF)
        sl = pl.ds(pl.multiple_of(i * GW, GW), GW)
        vp[:, sl] = gather_heads(dot(low, grads, NN))
        shaped = probs.reshape(GH, NEAR, TOK)
        prob_grad = dot(values, grads, NT).reshape(GH, NEAR, TOK)
        row_dot = jnp.sum(shaped * prob_grad, axis=1, keepdims=True)
        score_grad = (shaped * (prob_grad - row_dot)).reshape(GH * NEAR, TOK).astype(BF)
        turned_keys = dot(keys, turn, NN).astype(BF)
        part = SCALE * dot(score_grad, keys, TN)
        part_turned = SCALE * dot(score_grad, turned_keys, TN)
        qgrad[:, sl] = (part * cos_q() - part_turned * sin_q()).astype(BF)
        kp[:, sl] = gather_heads(SCALE * dot(score_grad, q_rot[i], NN))

    halo_out[0, 0:SPAN] = kp[2 * SPAN :, :]
    halo_out[0, SPAN:] = vp[2 * SPAN :, :]
    halo_out[1, 0:SPAN] = kp[0:SPAN, :]
    halo_out[1, SPAN:] = vp[0:SPAN, :]
    back = [
        remote(halo_out.at[0], halo_in.at[0], after),
        remote(halo_out.at[1], halo_in.at[1], before),
    ]

    project(far_block)

    for copy in y2_moves + x2_moves:
        copy.wait_recv()
    first = t1[y].astype(F32)
    second = t2[x].astype(F32)
    for m in range(3):
        first = first + p1[m].astype(F32)
        second = second + p2[m].astype(F32)
    u[:, :, 0:512] = first.astype(BF)
    u[:, :, 512:1024] = second.astype(BF)
    z_moves = [remote(u.at[flip(z, m, 3)], v.at[m - 1], z_peer[m - 1]) for m in range(1, 8)]

    project(far_pair_block)

    for copy in back:
        copy.wait_recv()
    vgrad_ref[...] = vp[SPAN : 2 * SPAN, :] + halo_in[0, SPAN:] + halo_in[1, SPAN:]
    key_total = kp[SPAN : 2 * SPAN, :] + halo_in[0, 0:SPAN] + halo_in[1, 0:SPAN]
    lane = lax.broadcasted_iota(jnp.int32, (SPAN, WIDTH), 1) % DH
    other = jnp.where(
        lane < HALF,
        -pltpu.roll(key_total, WIDTH - HALF, 1),
        pltpu.roll(key_total, HALF, 1),
    )
    wide_cos = jnp.concatenate([cos_k] * GROUPS, axis=1)
    wide_sin = jnp.concatenate([sin_k] * GROUPS, axis=1)
    kgrad_ref[...] = key_total * wide_cos - other * wide_sin

    for copy in z_moves:
        copy.wait_recv()
    total = u[z].astype(F32)
    for m in range(7):
        total = total + v[m].astype(F32)
    wgrad_ref[...] = total * factor

    for copy in started:
        copy.wait_send()


def finish(*refs):
    sems = refs[10]
    copies = [pltpu.make_async_copy(refs[i], refs[5 + i], sems.at[i]) for i in range(5)]
    for copy in copies:
        copy.start()
    for copy in copies:
        copy.wait()


def local(video_query, audio_key, audio_value, out_weight, grad_out, query_time, window):
    freqs = np.tile((10000.0 ** (-np.arange(HALF) / HALF)).astype(np.float32), 128 // HALF)
    factor = 1.0 / math.sqrt(TOK * lax.axis_size("ctx") * lax.axis_size("fsdp"))

    vmem = pl.BlockSpec(memory_space=pltpu.VMEM)
    hbm = pl.BlockSpec(memory_space=pl.ANY)
    n_sems = 56
    results = [
        ((TOK, 4 * WIDTH), BF),
        ((TOK, WIDTH), BF),
        ((SPAN, WIDTH), F32),
        ((SPAN, WIDTH), F32),
        ((16, WIDTH), F32),
    ]

    def body(*refs):
        kernel(factor, *refs)

    outs = pl.pallas_call(
        body,
        name="fused",
        out_shape=[pltpu.VMEM(shape, dtype) for shape, dtype in results],
        in_specs=[hbm, vmem, vmem, hbm, hbm, vmem, vmem, vmem],
        out_specs=[vmem] * 5,
        scratch_shapes=[
            pltpu.VMEM((GROUPS, TOK, GW), BF),
            pltpu.VMEM((GROUPS, TOK, GW), BF),
            pltpu.VMEM((3, 2 * SPAN, WIDTH), BF),
            pltpu.VMEM((4, WIDTH, WIDTH), BF),
            pltpu.VMEM((4, TOK, WIDTH), BF),
            pltpu.VMEM((2, TOK, WIDTH), BF),
            pltpu.VMEM((GROUPS, GH * NEAR, TOK), F32),
            pltpu.VMEM((GROUPS, TOK, GW), BF),
            pltpu.VMEM((WIDTH, TOK), BF),
            pltpu.VMEM((WIDTH, TOK), BF),
            pltpu.VMEM((2, TOK, 512), F32),
            pltpu.VMEM((GROUPS, TOK, GW), BF),
            pltpu.VMEM((TOK, 256), F32),
            pltpu.VMEM((NEAR, WIDTH), F32),
            pltpu.VMEM((NEAR, WIDTH), F32),
            pltpu.VMEM((2, 2 * SPAN, WIDTH), F32),
            pltpu.VMEM((2, 2 * SPAN, WIDTH), F32),
            pltpu.VMEM((4, 2, 8, 4, 16, 256), BF),
            pltpu.VMEM((2, 3, 8, 4, 16, 256), BF),
            pltpu.VMEM((4, 2, 2, 8, 2, 16, 256), BF),
            pltpu.VMEM((2, 3, 2, 8, 2, 16, 256), BF),
            pltpu.VMEM((4, 8, 16, 512), BF),
            pltpu.VMEM((3, 8, 16, 512), BF),
            pltpu.VMEM((4, 8, 16, 512), BF),
            pltpu.VMEM((3, 8, 16, 512), BF),
            pltpu.VMEM((8, 16, WIDTH), BF),
            pltpu.VMEM((7, 16, WIDTH), BF),
            pltpu.SemaphoreType.DMA((24,)),
            pltpu.SemaphoreType.DMA((n_sems,)),
            pltpu.SemaphoreType.DMA((n_sems,)),
        ],
        compiler_params=pltpu.CompilerParams(
            collective_id=0, has_side_effects=True, vmem_limit_bytes=46 << 20
        ),
    )(
        video_query[0],
        audio_key[0],
        audio_value[0],
        out_weight,
        grad_out[0],
        query_time.reshape(1, TOK),
        window,
        jnp.asarray(freqs).reshape(1, 128),
    )
    outs = pl.pallas_call(
        finish,
        name="finish",
        out_shape=[jax.ShapeDtypeStruct(shape, dtype) for shape, dtype in results],
        in_specs=[vmem] * 5,
        out_specs=[hbm] * 5,
        scratch_shapes=[pltpu.SemaphoreType.DMA((5,))],
    )(*outs)
    output, query_grad, key_grad, value_grad, weight_grad = outs
    return (output[None], query_grad[None], key_grad[None], value_grad[None], weight_grad)


def solution(mesh):
    in_specs = (
        P("fsdp", "ctx", None),
        P("fsdp", "ctx", None),
        P("fsdp", "ctx", None),
        P(None, "fsdp"),
        P("fsdp", "ctx", None),
        P("ctx"),
        P(None, "ctx"),
    )
    out_specs = (
        P("fsdp", "ctx", None),
        P("fsdp", "ctx", None),
        P("fsdp", "ctx", None),
        P("fsdp", "ctx", None),
        P("ctx", "fsdp"),
    )
    return jax.shard_map(local, mesh=mesh, in_specs=in_specs, out_specs=out_specs, check_vma=False)
```

```python
import math

import jax
import jax.numpy as jnp
import numpy as np
from jax import lax
from jax.experimental import pallas as pl
from jax.experimental.pallas import tpu as pltpu
from jax.sharding import PartitionSpec as P

DH = 64
HALF = DH // 2
TOK = 512
WIDTH = 1024
SPAN = 8
NEAR = 3 * SPAN
GROUPS = 4
GW = WIDTH // GROUPS
GH = GW // DH
SCALE = 1.0 / math.sqrt(DH)
MESH = pl.DeviceIdType.MESH
BF = jnp.bfloat16
F32 = jnp.float32

NN = (((1,), (0,)), ((), ()))
NT = (((1,), (1,)), ((), ()))
TN = (((0,), (0,)), ((), ()))


def dot(a, b, dims):
    return lax.dot_general(a, b, dims, preferred_element_type=F32)


def flip(value, mask, bits):
    out = 0
    for bit in range(bits):
        digit = (value // (1 << bit)) % 2
        if (mask >> bit) & 1:
            digit = 1 - digit
        out = out + digit * (1 << bit)
    return out


def kernel(
    factor,
    query_hbm,
    key_hbm,
    value_hbm,
    weight_hbm,
    grad_hbm,
    time_hbm,
    window_hbm,
    freq_hbm,
    out_stage,
    qgrad,
    kgrad_ref,
    vgrad_ref,
    wgrad_ref,
    key_ref,
    value_ref,
    time_ref,
    window_ref,
    freq_ref,
    q_raw,
    q_rot,
    near_kv,
    w_all,
    g_own,
    g_pair,
    probs_s,
    att,
    att_t,
    att_t_pair,
    ag32,
    ag,
    table,
    kp,
    vp,
    halo_out,
    halo_in,
    s1,
    r1,
    s2,
    r2,
    t1,
    p1,
    t2,
    p2,
    u,
    v,
    loc,
    sem_s,
    sem_r,
):
    ctx = lax.axis_index("ctx")
    fs = lax.axis_index("fsdp")
    z = ctx // 8
    y = (ctx // 2) % 4
    xl = ctx % 2
    xh = fs // 2
    core = fs % 2
    x = xh * 2 + xl
    n_ctx = 64

    def device(x_, y_, z_, core_):
        return (z_ * 8 + y_ * 2 + x_ % 2, (x_ // 2) * 2 + core_)

    pair = (ctx, xh * 2 + 1 - core)
    after = ((ctx + 1) % n_ctx, fs)
    before = ((ctx + n_ctx - 1) % n_ctx, fs)
    x_peer = [device(flip(x, m, 2), y, z, core) for m in (1, 2, 3)]
    y_peer = [device(x, flip(y, m, 2), z, core) for m in (1, 2, 3)]
    z_peer = [device(x, y, flip(z, m, 3), core) for m in range(1, 8)]
    z_step = {d: device(x, y, (z + d + 8) % 8, core) for d in (1, -1, 2, -2)}
    y_step = {d: device(x, (y + d + 4) % 4, z, core) for d in (1, -1)}

    counter = [0]

    def remote(src, dst, target):
        index = counter[0]
        counter[0] += 1
        copy = pltpu.make_async_remote_copy(
            src_ref=src,
            dst_ref=dst,
            send_sem=sem_s.at[index],
            recv_sem=sem_r.at[index],
            device_id=target,
            device_id_type=MESH,
        )
        copy.start()
        started.append(copy)
        return copy

    started = []
    local_counter = [0]

    def local(src, dst):
        index = local_counter[0]
        local_counter[0] += 1
        copy = pltpu.make_async_copy(src, dst, loc.at[index])
        copy.start()
        return copy

    block = fs
    pair_block = xh * 2 + 1 - core
    far_block = (1 - xh) * 2 + core
    far_pair_block = (1 - xh) * 2 + 1 - core
    small = [
        local(freq_hbm, freq_ref),
        local(time_hbm, time_ref),
        local(window_hbm, window_ref),
        local(key_hbm, key_ref),
        local(value_hbm, value_ref),
    ]
    load_q = [local(query_hbm.at[:, pl.ds(i * GW, GW)], q_raw.at[i]) for i in range(GROUPS)]
    load_g = [local(grad_hbm.at[:, pl.ds(i * WIDTH, WIDTH)], g_own.at[i]) for i in range(4)]
    load_w = local(weight_hbm, w_all.at[block])

    barrier = pltpu.get_barrier_semaphore()
    greet = [pair, after, before] + x_peer + y_peer + z_peer
    for target in greet:
        pl.semaphore_signal(barrier, inc=1, device_id=target, device_id_type=MESH)

    for copy in small:
        copy.wait()

    lane_i = lax.broadcasted_iota(jnp.int32, (GW, GW), 0)
    lane_j = lax.broadcasted_iota(jnp.int32, (GW, GW), 1)
    first_j = lane_j % DH < HALF
    turn = jnp.where(
        first_j & (lane_i == lane_j + HALF),
        -1.0,
        jnp.where((~first_j) & (lane_i == lane_j - HALF), 1.0, 0.0),
    ).astype(BF)
    near_row = lax.broadcasted_iota(jnp.int32, (32, 1), 0) + ctx * SPAN - SPAN
    angles = near_row.astype(F32) * freq_ref[...]
    near_table = jnp.concatenate([jnp.cos(angles), jnp.sin(angles)], axis=1)
    pieces = []
    rest = near_table
    for _ in range(3):
        piece = rest.astype(BF).astype(F32)
        pieces.append(piece)
        rest = rest - piece
    time_row = jnp.where(near_row == time_ref[...], 1.0, 0.0)
    chosen = jnp.concatenate([time_row] * 3, axis=0).astype(BF)
    table[...] = dot(chosen, jnp.concatenate(pieces, axis=0).astype(BF), TN)

    def cos_q():
        return jnp.concatenate([table[:, :128]] * 2, axis=1)

    def sin_q():
        return jnp.concatenate([table[:, 128:]] * 2, axis=1)

    cos_k = jnp.concatenate([near_table[SPAN : 2 * SPAN, :128]] * 2, axis=1)
    sin_k = jnp.concatenate([near_table[SPAN : 2 * SPAN, 128:]] * 2, axis=1)
    for i in range(GROUPS):
        sl = slice(i * GW, (i + 1) * GW)
        raw = key_ref[:, sl]
        turned = raw.astype(F32) * cos_k + dot(raw, turn, NN) * sin_k
        near_kv[0, :, sl] = jnp.concatenate([turned, value_ref[:, sl].astype(F32)], axis=0).astype(BF)

    pl.semaphore_wait(barrier, len(greet))

    halo_a = remote(near_kv.at[0], near_kv.at[1], after)
    halo_b = remote(near_kv.at[0], near_kv.at[2], before)
    quarter = (z + 2 * (y % 2)) % 4
    cross = []
    for half in range(2):
        rows = pl.ds(quarter * 256 + half * 128, 128)
        cross.append(remote(weight_hbm.at[rows], w_all.at[block, rows], x_peer[2]))
    pair_g = [
        remote(
            grad_hbm.at[:, pl.ds(pl.multiple_of((2 * h + 1 - core) * WIDTH, WIDTH), WIDTH)],
            g_pair.at[h],
            pair,
        )
        for h in range(2)
    ]

    for copy in load_q:
        copy.wait()

    @pl.loop(0, GROUPS)
    def _(i):
        raw = q_raw[i]
        q_rot[i] = (raw.astype(F32) * cos_q() + dot(raw, turn, NN) * sin_q()).astype(BF)

    def early(j):
        rows = pl.ds(j * 512, 512)
        ag32[j] = dot(g_own[block], w_all[block, rows, :], NT)

    for copy in load_g:
        copy.wait()
    load_w.wait()
    early(0)

    halo_a.wait_recv()
    halo_b.wait_recv()

    near_index = (
        lax.broadcasted_iota(jnp.int32, (NEAR, TOK), 0) + ctx * SPAN - SPAN
    )
    allowed = (near_index >= window_ref[0:1, :]) & (near_index < window_ref[1:2, :])
    head_row = lax.broadcasted_iota(jnp.int32, (GH, NEAR, GW), 0)
    head_col = lax.broadcasted_iota(jnp.int32, (GH, NEAR, GW), 2) // DH
    own_head = head_row == head_col

    def spread(row, i):
        sl = pl.ds(pl.multiple_of(i * GW, GW), GW)
        parts = [near_kv[slot, :, sl].astype(F32)[row : row + SPAN] for slot in (1, 0, 2)]
        near = jnp.concatenate(parts, axis=0)
        wide = jnp.where(own_head, near[None], 0.0)
        return wide.reshape(GH * NEAR, GW).astype(BF)

    def gather_heads(wide):
        shaped = wide.reshape(GH, NEAR, GW)
        return jnp.sum(jnp.where(own_head, shaped, 0.0), axis=0)

    pair_a = []
    for i in range(GROUPS):
        keys = spread(0, i)
        values = spread(SPAN, i)
        scores = SCALE * dot(keys, q_rot[i], NT).reshape(GH, NEAR, TOK)
        masked = jnp.where(allowed[None], scores, -1e30)
        highest = jnp.max(masked, axis=1, keepdims=True)
        expo = jnp.where(allowed[None], jnp.exp(masked - highest), 0.0)
        probs = (expo / jnp.sum(expo, axis=1, keepdims=True)).reshape(GH * NEAR, TOK)
        probs_s[i] = probs
        low = probs.astype(BF)
        rows = pl.ds(i * GW, GW)
        att_t[rows, :] = dot(values, low, TN).astype(BF)
        pair_a.append(remote(att_t.at[rows], att_t_pair.at[rows], pair))
        att[i] = dot(low, values, TN).astype(BF)

    pair_w = remote(weight_hbm, w_all.at[block], pair)
    early(1)

    far_moves = []

    def pass_on(half):
        cross[half].wait_recv()
        start = quarter * 256 + half * 128
        piece = w_all.at[far_block, pl.ds(start, 128)]
        one = w_all.at[far_block, pl.ds(start, 64)]
        two = w_all.at[far_block, pl.ds(start + 64, 64)]
        up, down = (y_step[1], y_step[-1]) if half == 0 else (z_step[2], z_step[-2])
        moves = [
            remote(piece, piece, z_step[1]),
            remote(piece, piece, z_step[-1]),
            remote(one, one, up),
            remote(two, two, down),
            remote(piece, piece, pair),
        ]
        far_moves.append(moves)

    def hand_over(half):
        for k, step in ((0, 3), (1, 1), (2, 2)):
            far_moves[half][k].wait_recv()
            if k == 2:
                far_moves[half][3].wait_recv()
            rows = pl.ds(((quarter + step) % 4) * 256 + half * 128, 128)
            piece = w_all.at[far_block, rows]
            far_moves[half].append(remote(piece, piece, pair))

    pass_on(0)

    for copy in pair_g + pair_a:
        copy.wait_recv()

    def gradient(h, part, store):
        cols = slice(part * 512, (part + 1) * 512)

        @pl.loop(0, 2)
        def _(i):
            rows = pl.ds(pl.multiple_of(i * 512, 512), 512)
            total = dot(att_t[rows, :], g_own[2 * h + core, :, cols], NN)
            total = total + dot(att_t_pair[rows, :], g_pair[h, :, cols], NN)
            store(i, total.astype(BF).reshape(4, 4, 2, 16, 512))

    def store_x(h):
        def store(i, total):
            for low_x in range(2):
                for k in range(2):
                    s1[2 * h + low_x, k, pl.ds(i * 4, 4)] = total[:, :, low_x, :, k * 256 : k * 256 + 256]

        return store

    def store_y(h):
        def store(i, total):
            for to_y in range(4):
                for k in range(2):
                    s2[to_y, k, h, pl.ds(i * 4, 4)] = total[:, to_y, :, :, k * 256 : k * 256 + 256]

        return store

    near = (1, 3)
    x_first = {}
    y_first = {}

    def send_x(k, slot):
        to = flip(x, 2 if slot == 0 else near[k], 2)
        x_first[k, slot] = remote(s1.at[to, k], r1.at[k, slot], x_peer[near[k] - 1])

    def send_y(k, slot, h):
        to = flip(y, 2 if slot == 0 else near[k], 2)
        y_first[k, slot, h] = remote(s2.at[to, k, h], r2.at[k, slot, h], y_peer[near[k] - 1])

    gradient(1 - xh, 0, store_x(1 - xh))
    send_x(1, 0)
    send_x(0, 0)
    send_x(1, 1)
    gradient(0, 1, store_y(0))
    for k in range(2):
        send_y(k, 0, 0)
    gradient(1, 1, store_y(1))
    for k in range(2):
        send_y(k, 0, 1)
    for h in range(2):
        for k in range(2):
            send_y(k, 1, h)
    pass_on(1)
    gradient(xh, 0, store_x(xh))
    send_x(0, 1)

    pair_w.wait_recv()

    def project(b):
        @pl.loop(0, 2)
        def _(j):
            cols = pl.ds(pl.multiple_of(j * 512, 512), 512)
            out_cols = pl.ds(pl.multiple_of(b * WIDTH + j * 512, 512), 512)
            total = dot(att[0], w_all[b, 0:GW, cols], NN)
            for i in range(1, GROUPS):
                total = total + dot(att[i], w_all[b, i * GW : (i + 1) * GW, cols], NN)
            out_stage[:, out_cols] = total.astype(BF)

    @pl.loop(0, 2)
    def _(j):
        rows = pl.ds(pl.multiple_of(j * 512, 512), 512)
        ag32[j] += dot(g_own[pair_block], w_all[pair_block, rows, :], NT)

    x_second = []
    y_second = []
    for k in range(2):
        to = flip(x, near[1 - k], 2)
        x_first[k, 0].wait_recv()

        @pl.loop(0, 4)
        def _(i):
            part = pl.ds(i * 2, 2)
            s1[to, k, part] = (s1[to, k, part].astype(F32) + r1[k, 0, part].astype(F32)).astype(BF)

        x_second.append(remote(s1.at[to, k], r1.at[k, 2], x_peer[near[1 - k] - 1]))

    project(block)

    for k in range(2):
        to = flip(y, near[1 - k], 2)
        for h in range(2):
            y_first[k, 0, h].wait_recv()

            @pl.loop(0, 2)
            def _(i):
                part = pl.ds(i * 4, 4)
                s2[to, k, h, part] = (
                    s2[to, k, h, part].astype(F32) + r2[k, 0, h, part].astype(F32)
                ).astype(BF)

        y_second.append(remote(s2.at[to, k], r2.at[k, 2], y_peer[near[1 - k] - 1]))

    project(pair_block)
    hand_over(0)

    for k in range(2):
        x_first[k, 1].wait_recv()
        x_second[k].wait_recv()

    @pl.loop(0, 4)
    def _(to_y):
        for k in range(2):
            total = s1[x, k, :, to_y].astype(F32)
            for m in (1, 2):
                total = total + r1[k, m, :, to_y].astype(F32)
            t1[to_y, :, :, k * 256 : k * 256 + 256] = total.astype(BF)

    y2_moves = [remote(t1.at[flip(y, m, 2)], p1.at[m - 1], y_peer[m - 1]) for m in (1, 2, 3)]
    for k in range(2):
        for h in range(2):
            y_first[k, 1, h].wait_recv()
        y_second[k].wait_recv()

    @pl.loop(0, 4)
    def _(to_x):
        h = to_x // 2
        low_x = to_x % 2
        for k in range(2):
            total = s2[y, k, h, :, low_x].astype(F32)
            for m in (1, 2):
                total = total + r2[k, m, h, :, low_x].astype(F32)
            t2[to_x, :, :, k * 256 : k * 256 + 256] = total.astype(BF)

    x2_moves = [remote(t2.at[flip(x, m, 2)], p2.at[m - 1], x_peer[m - 1]) for m in (1, 2, 3)]

    hand_over(1)
    for half in range(2):
        for k in range(4, 8):
            far_moves[half][k].wait_recv()

    @pl.loop(0, 2)
    def _(j):
        rows = pl.ds(pl.multiple_of(j * 512, 512), 512)
        total = ag32[j] + dot(g_own[far_block], w_all[far_block, rows, :], NT)
        total = total + dot(g_own[far_pair_block], w_all[far_pair_block, rows, :], NT)
        low = total.astype(BF)
        ag[2 * j] = low[:, :GW]
        ag[2 * j + 1] = low[:, GW:]

    @pl.loop(0, GROUPS)
    def _(i):
        keys = spread(0, i)
        values = spread(SPAN, i)
        grads = ag[i]
        probs = probs_s[i]
        low = probs.astype(BF)
        sl = pl.ds(pl.multiple_of(i * GW, GW), GW)
        vp[:, sl] = gather_heads(dot(low, grads, NN))
        shaped = probs.reshape(GH, NEAR, TOK)
        prob_grad = dot(values, grads, NT).reshape(GH, NEAR, TOK)
        row_dot = jnp.sum(shaped * prob_grad, axis=1, keepdims=True)
        score_grad = (shaped * (prob_grad - row_dot)).reshape(GH * NEAR, TOK).astype(BF)
        turned_keys = dot(keys, turn, NN).astype(BF)
        part = SCALE * dot(score_grad, keys, TN)
        part_turned = SCALE * dot(score_grad, turned_keys, TN)
        qgrad[:, sl] = (part * cos_q() - part_turned * sin_q()).astype(BF)
        kp[:, sl] = gather_heads(SCALE * dot(score_grad, q_rot[i], NN))

    halo_out[0, 0:SPAN] = kp[2 * SPAN :, :]
    halo_out[0, SPAN:] = vp[2 * SPAN :, :]
    halo_out[1, 0:SPAN] = kp[0:SPAN, :]
    halo_out[1, SPAN:] = vp[0:SPAN, :]
    back = [
        remote(halo_out.at[0], halo_in.at[0], after),
        remote(halo_out.at[1], halo_in.at[1], before),
    ]

    project(far_block)

    for copy in y2_moves + x2_moves:
        copy.wait_recv()
    first = t1[y].astype(F32)
    second = t2[x].astype(F32)
    for m in range(3):
        first = first + p1[m].astype(F32)
        second = second + p2[m].astype(F32)
    u[:, :, 0:512] = first.astype(BF)
    u[:, :, 512:1024] = second.astype(BF)
    z_moves = [remote(u.at[flip(z, m, 3)], v.at[m - 1], z_peer[m - 1]) for m in range(1, 8)]

    project(far_pair_block)

    for copy in back:
        copy.wait_recv()
    vgrad_ref[...] = vp[SPAN : 2 * SPAN, :] + halo_in[0, SPAN:] + halo_in[1, SPAN:]
    key_total = kp[SPAN : 2 * SPAN, :] + halo_in[0, 0:SPAN] + halo_in[1, 0:SPAN]
    lane = lax.broadcasted_iota(jnp.int32, (SPAN, WIDTH), 1) % DH
    other = jnp.where(
        lane < HALF,
        -pltpu.roll(key_total, WIDTH - HALF, 1),
        pltpu.roll(key_total, HALF, 1),
    )
    wide_cos = jnp.concatenate([cos_k] * GROUPS, axis=1)
    wide_sin = jnp.concatenate([sin_k] * GROUPS, axis=1)
    kgrad_ref[...] = key_total * wide_cos - other * wide_sin

    for copy in z_moves:
        copy.wait_recv()
    total = u[z].astype(F32)
    for m in range(7):
        total = total + v[m].astype(F32)
    wgrad_ref[...] = total * factor

    for copy in started:
        copy.wait_send()


def finish(*refs):
    sems = refs[10]
    copies = [pltpu.make_async_copy(refs[i], refs[5 + i], sems.at[i]) for i in range(5)]
    for copy in copies:
        copy.start()
    for copy in copies:
        copy.wait()


def local(video_query, audio_key, audio_value, out_weight, grad_out, query_time, window):
    freqs = np.tile((10000.0 ** (-np.arange(HALF) / HALF)).astype(np.float32), 128 // HALF)
    factor = 1.0 / math.sqrt(TOK * lax.axis_size("ctx") * lax.axis_size("fsdp"))

    vmem = pl.BlockSpec(memory_space=pltpu.VMEM)
    hbm = pl.BlockSpec(memory_space=pltpu.HBM)
    n_sems = 58
    results = [
        ((TOK, 4 * WIDTH), BF),
        ((TOK, WIDTH), BF),
        ((SPAN, WIDTH), F32),
        ((SPAN, WIDTH), F32),
        ((16, WIDTH), F32),
    ]

    inputs = (
        video_query[0],
        audio_key[0],
        audio_value[0],
        out_weight,
        grad_out[0],
        query_time.reshape(1, TOK),
        window,
        jnp.asarray(freqs).reshape(1, 128),
    )

    def body(*refs):
        kernel(factor, *refs)

    outs = pl.pallas_call(
        body,
        name="fused",
        out_shape=[pltpu.VMEM(shape, dtype) for shape, dtype in results],
        in_specs=[hbm] * 8,
        out_specs=[vmem] * 5,
        scratch_shapes=[
            pltpu.VMEM((SPAN, WIDTH), BF),
            pltpu.VMEM((SPAN, WIDTH), BF),
            pltpu.VMEM((1, TOK), jnp.int32),
            pltpu.VMEM((2, TOK), jnp.int32),
            pltpu.VMEM((1, 128), F32),
            pltpu.VMEM((GROUPS, TOK, GW), BF),
            pltpu.VMEM((GROUPS, TOK, GW), BF),
            pltpu.VMEM((3, 2 * SPAN, WIDTH), BF),
            pltpu.VMEM((4, WIDTH, WIDTH), BF),
            pltpu.VMEM((4, TOK, WIDTH), BF),
            pltpu.VMEM((2, TOK, WIDTH), BF),
            pltpu.VMEM((GROUPS, GH * NEAR, TOK), F32),
            pltpu.VMEM((GROUPS, TOK, GW), BF),
            pltpu.VMEM((WIDTH, TOK), BF),
            pltpu.VMEM((WIDTH, TOK), BF),
            pltpu.VMEM((2, TOK, 512), F32),
            pltpu.VMEM((GROUPS, TOK, GW), BF),
            pltpu.VMEM((TOK, 256), F32),
            pltpu.VMEM((NEAR, WIDTH), F32),
            pltpu.VMEM((NEAR, WIDTH), F32),
            pltpu.VMEM((2, 2 * SPAN, WIDTH), F32),
            pltpu.VMEM((2, 2 * SPAN, WIDTH), F32),
            pltpu.VMEM((4, 2, 8, 4, 16, 256), BF),
            pltpu.VMEM((2, 3, 8, 4, 16, 256), BF),
            pltpu.VMEM((4, 2, 2, 8, 2, 16, 256), BF),
            pltpu.VMEM((2, 3, 2, 8, 2, 16, 256), BF),
            pltpu.VMEM((4, 8, 16, 512), BF),
            pltpu.VMEM((3, 8, 16, 512), BF),
            pltpu.VMEM((4, 8, 16, 512), BF),
            pltpu.VMEM((3, 8, 16, 512), BF),
            pltpu.VMEM((8, 16, WIDTH), BF),
            pltpu.VMEM((7, 16, WIDTH), BF),
            pltpu.SemaphoreType.DMA((24,)),
            pltpu.SemaphoreType.DMA((n_sems,)),
            pltpu.SemaphoreType.DMA((n_sems,)),
        ],
        compiler_params=pltpu.CompilerParams(
            collective_id=0, has_side_effects=True, vmem_limit_bytes=46 << 20
        ),
    )(
        *[pltpu.with_memory_space_constraint(arg, pltpu.HBM) for arg in inputs]
    )
    outs = pl.pallas_call(
        finish,
        name="finish",
        out_shape=[jax.ShapeDtypeStruct(shape, dtype) for shape, dtype in results],
        in_specs=[vmem] * 5,
        out_specs=[hbm] * 5,
        scratch_shapes=[pltpu.SemaphoreType.DMA((5,))],
        compiler_params=pltpu.CompilerParams(vmem_limit_bytes=4 << 20),
    )(*[pltpu.with_memory_space_constraint(out, pltpu.VMEM) for out in outs])
    output, query_grad, key_grad, value_grad, weight_grad = outs
    return (output[None], query_grad[None], key_grad[None], value_grad[None], weight_grad)


def solution(mesh):
    in_specs = (
        P("fsdp", "ctx", None),
        P("fsdp", "ctx", None),
        P("fsdp", "ctx", None),
        P(None, "fsdp"),
        P("fsdp", "ctx", None),
        P("ctx"),
        P(None, "ctx"),
    )
    out_specs = (
        P("fsdp", "ctx", None),
        P("fsdp", "ctx", None),
        P("fsdp", "ctx", None),
        P("fsdp", "ctx", None),
        P("ctx", "fsdp"),
    )
    return jax.shard_map(local, mesh=mesh, in_specs=in_specs, out_specs=out_specs, check_vma=False)
```

```python
import math

import jax
import jax.numpy as jnp
import numpy as np
from jax import lax
from jax.experimental import pallas as pl
from jax.experimental.pallas import tpu as pltpu
from jax.sharding import PartitionSpec as P

DH = 64
HALF = DH // 2
TOK = 512
WIDTH = 1024
SPAN = 8
NEAR = 3 * SPAN
GROUPS = 4
GW = WIDTH // GROUPS
GH = GW // DH
SCALE = 1.0 / math.sqrt(DH)
MESH = pl.DeviceIdType.MESH
BF = jnp.bfloat16
F32 = jnp.float32

NN = (((1,), (0,)), ((), ()))
NT = (((1,), (1,)), ((), ()))
TN = (((0,), (0,)), ((), ()))


def dot(a, b, dims):
    return lax.dot_general(a, b, dims, preferred_element_type=F32)


def flip(value, mask, bits):
    out = 0
    for bit in range(bits):
        digit = (value // (1 << bit)) % 2
        if (mask >> bit) & 1:
            digit = 1 - digit
        out = out + digit * (1 << bit)
    return out


def kernel(
    factor,
    query_hbm,
    key_hbm,
    value_hbm,
    weight_hbm,
    grad_hbm,
    time_hbm,
    window_hbm,
    freq_hbm,
    out_stage,
    qgrad,
    kgrad_ref,
    vgrad_ref,
    wgrad_ref,
    key_ref,
    value_ref,
    time_ref,
    window_ref,
    freq_ref,
    q_raw,
    q_rot,
    near_kv,
    w_all,
    g_own,
    g_pair,
    keys_s,
    values_s,
    probs_s,
    att,
    att_t,
    att_t_pair,
    ag32,
    ag,
    table,
    kp,
    vp,
    halo_out,
    halo_in,
    s1,
    r1,
    s2,
    r2,
    t1,
    p1,
    t2,
    p2,
    u,
    v,
    loc,
    sem_s,
    sem_r,
):
    ctx = lax.axis_index("ctx")
    fs = lax.axis_index("fsdp")
    z = ctx // 8
    y = (ctx // 2) % 4
    xl = ctx % 2
    xh = fs // 2
    core = fs % 2
    x = xh * 2 + xl
    n_ctx = 64

    def device(x_, y_, z_, core_):
        return (z_ * 8 + y_ * 2 + x_ % 2, (x_ // 2) * 2 + core_)

    pair = (ctx, xh * 2 + 1 - core)
    after = ((ctx + 1) % n_ctx, fs)
    before = ((ctx + n_ctx - 1) % n_ctx, fs)
    x_peer = [device(flip(x, m, 2), y, z, core) for m in (1, 2, 3)]
    y_peer = [device(x, flip(y, m, 2), z, core) for m in (1, 2, 3)]
    z_peer = [device(x, y, flip(z, m, 3), core) for m in range(1, 8)]
    z_step = {d: device(x, y, (z + d + 8) % 8, core) for d in (1, -1, 2, -2)}
    y_step = {d: device(x, (y + d + 4) % 4, z, core) for d in (1, -1)}

    barrier = pltpu.get_barrier_semaphore()
    greet = [pair, after, before] + x_peer + y_peer + z_peer
    for target in greet:
        pl.semaphore_signal(barrier, inc=1, device_id=target, device_id_type=MESH)

    counter = [0]

    def remote(src, dst, target):
        index = counter[0]
        counter[0] += 1
        copy = pltpu.make_async_remote_copy(
            src_ref=src,
            dst_ref=dst,
            send_sem=sem_s.at[index],
            recv_sem=sem_r.at[index],
            device_id=target,
            device_id_type=MESH,
        )
        copy.start()
        started.append(copy)
        return copy

    started = []
    local_counter = [0]

    def local(src, dst):
        index = local_counter[0]
        local_counter[0] += 1
        copy = pltpu.make_async_copy(src, dst, loc.at[index])
        copy.start()
        return copy

    block = fs
    pair_block = xh * 2 + 1 - core
    far_block = (1 - xh) * 2 + core
    far_pair_block = (1 - xh) * 2 + 1 - core
    small = [
        local(freq_hbm, freq_ref),
        local(time_hbm, time_ref),
        local(window_hbm, window_ref),
        local(key_hbm, key_ref),
        local(value_hbm, value_ref),
    ]
    load_q = [local(query_hbm.at[:, pl.ds(i * GW, GW)], q_raw.at[i]) for i in range(GROUPS)]
    load_g = [local(grad_hbm.at[:, pl.ds(i * WIDTH, WIDTH)], g_own.at[i]) for i in range(4)]
    load_w = local(weight_hbm, w_all.at[block])

    for copy in small:
        copy.wait()

    lane = lax.broadcasted_iota(jnp.int32, (SPAN, WIDTH), 1) % DH

    def turned(values):
        left = pltpu.roll(values, WIDTH - HALF, 1)
        right = pltpu.roll(values, HALF, 1)
        return jnp.where(lane < HALF, -left, right)

    own_row = lax.broadcasted_iota(jnp.int32, (SPAN, 1), 0) + ctx * SPAN
    own_angles = own_row.astype(F32) * freq_ref[...]
    cos_k = jnp.concatenate([jnp.cos(own_angles)] * (WIDTH // 128), axis=1)
    sin_k = jnp.concatenate([jnp.sin(own_angles)] * (WIDTH // 128), axis=1)
    raw_k = key_ref[...].astype(F32)
    near_kv[0] = jnp.concatenate(
        [raw_k * cos_k + turned(raw_k) * sin_k, value_ref[...].astype(F32)], axis=0
    ).astype(BF)

    pl.semaphore_wait(barrier, len(greet))

    halo_a = remote(near_kv.at[0], near_kv.at[1], after)
    halo_b = remote(near_kv.at[0], near_kv.at[2], before)
    quarter = (z + 2 * (y % 2)) % 4
    cross = []
    for half in range(2):
        rows = pl.ds(quarter * 256 + half * 128, 128)
        cross.append(remote(weight_hbm.at[rows], w_all.at[block, rows], x_peer[2]))
    pair_g = [
        remote(
            grad_hbm.at[:, pl.ds(pl.multiple_of((2 * h + 1 - core) * WIDTH, WIDTH), WIDTH)],
            g_pair.at[h],
            pair,
        )
        for h in range(2)
    ]

    near_row = lax.broadcasted_iota(jnp.int32, (32, 1), 0) + ctx * SPAN - SPAN
    angles = near_row.astype(F32) * freq_ref[...]
    near_table = jnp.concatenate([jnp.cos(angles), jnp.sin(angles)], axis=1)
    pieces = []
    rest = near_table
    for _ in range(3):
        piece = rest.astype(BF).astype(F32)
        pieces.append(piece)
        rest = rest - piece
    time_row = jnp.where(near_row == time_ref[...], 1.0, 0.0)
    chosen = jnp.concatenate([time_row] * 3, axis=0).astype(BF)
    table[...] = dot(chosen, jnp.concatenate(pieces, axis=0).astype(BF), TN)

    def cos_q():
        return jnp.concatenate([table[:, :128]] * 2, axis=1)

    def sin_q():
        return jnp.concatenate([table[:, 128:]] * 2, axis=1)

    lane_i = lax.broadcasted_iota(jnp.int32, (GW, GW), 0)
    lane_j = lax.broadcasted_iota(jnp.int32, (GW, GW), 1)
    first_j = lane_j % DH < HALF
    turn = jnp.where(
        first_j & (lane_i == lane_j + HALF),
        -1.0,
        jnp.where((~first_j) & (lane_i == lane_j - HALF), 1.0, 0.0),
    ).astype(BF)
    for copy in load_q:
        copy.wait()

    @pl.loop(0, GROUPS)
    def _(i):
        raw = q_raw[i]
        q_rot[i] = (raw.astype(F32) * cos_q() + dot(raw, turn, NN) * sin_q()).astype(BF)

    def early(j):
        rows = pl.ds(j * 512, 512)
        ag32[j] = dot(g_own[block], w_all[block, rows, :], NT)

    for copy in load_g:
        copy.wait()
    load_w.wait()
    early(0)

    halo_a.wait_recv()
    halo_b.wait_recv()

    near_index = (
        lax.broadcasted_iota(jnp.int32, (NEAR, TOK), 0) + ctx * SPAN - SPAN
    )
    allowed = (near_index >= window_ref[0:1, :]) & (near_index < window_ref[1:2, :])
    head_row = lax.broadcasted_iota(jnp.int32, (GH, NEAR, GW), 0)
    head_col = lax.broadcasted_iota(jnp.int32, (GH, NEAR, GW), 2) // DH
    own_head = head_row == head_col

    def spread(row, i):
        sl = pl.ds(pl.multiple_of(i * GW, GW), GW)
        parts = [near_kv[slot, :, sl].astype(F32)[row : row + SPAN] for slot in (1, 0, 2)]
        near = jnp.concatenate(parts, axis=0)
        wide = jnp.where(own_head, near[None], 0.0)
        return wide.reshape(GH * NEAR, GW).astype(BF)

    def gather_heads(wide):
        shaped = wide.reshape(GH, NEAR, GW)
        return jnp.sum(jnp.where(own_head, shaped, 0.0), axis=0)

    pair_a = []
    for i in range(GROUPS):
        keys = spread(0, i)
        values = spread(SPAN, i)
        keys_s[i] = keys
        values_s[i] = values
        scores = SCALE * dot(keys, q_rot[i], NT).reshape(GH, NEAR, TOK)
        masked = jnp.where(allowed[None], scores, -1e30)
        highest = jnp.max(masked, axis=1, keepdims=True)
        expo = jnp.where(allowed[None], jnp.exp(masked - highest), 0.0)
        probs = (expo / jnp.sum(expo, axis=1, keepdims=True)).reshape(GH * NEAR, TOK)
        probs_s[i] = probs
        low = probs.astype(BF)
        rows = pl.ds(i * GW, GW)
        att_t[rows, :] = dot(values, low, TN).astype(BF)
        pair_a.append(remote(att_t.at[rows], att_t_pair.at[rows], pair))

    pair_w = remote(weight_hbm, w_all.at[block], pair)
    early(1)

    far_moves = []

    def pass_on(half):
        cross[half].wait_recv()
        start = quarter * 256 + half * 128
        piece = w_all.at[far_block, pl.ds(start, 128)]
        one = w_all.at[far_block, pl.ds(start, 64)]
        two = w_all.at[far_block, pl.ds(start + 64, 64)]
        up, down = (y_step[1], y_step[-1]) if half == 0 else (z_step[2], z_step[-2])
        moves = [
            remote(piece, piece, z_step[1]),
            remote(piece, piece, z_step[-1]),
            remote(one, one, up),
            remote(two, two, down),
            remote(piece, piece, pair),
        ]
        far_moves.append(moves)

    def hand_over(half):
        for k, step in ((0, 3), (1, 1), (2, 2)):
            far_moves[half][k].wait_recv()
            if k == 2:
                far_moves[half][3].wait_recv()
            rows = pl.ds(((quarter + step) % 4) * 256 + half * 128, 128)
            piece = w_all.at[far_block, rows]
            far_moves[half].append(remote(piece, piece, pair))

    pass_on(0)

    for copy in pair_g + pair_a[:2]:
        copy.wait_recv()

    def gradient(h, part, i, store):
        cols = slice(part * 512, (part + 1) * 512)
        rows = slice(i * 512, (i + 1) * 512)
        total = dot(att_t[rows, :], g_own[2 * h + core, :, cols], NN)
        total = total + dot(att_t_pair[rows, :], g_pair[h, :, cols], NN)
        store(h, i, total.astype(BF).reshape(4, 4, 2, 16, 512))

    def store_x(h, i, total):
        for low_x in range(2):
            for k in range(2):
                s1[2 * h + low_x, k, i] = total[:, :, low_x, :, k * 256 : k * 256 + 256]

    def store_y(h, i, total):
        for to_y in range(4):
            for k in range(2):
                s2[to_y, k, i, h] = total[:, to_y, :, :, k * 256 : k * 256 + 256]

    near = (1, 3)
    x_first = {}
    y_first = {}

    def send_x(k, slot, i):
        to = flip(x, 2 if slot == 0 else near[k], 2)
        x_first[k, slot, i] = remote(s1.at[to, k, i], r1.at[k, slot, i], x_peer[near[k] - 1])

    def send_y(k, slot, i, h=None):
        to = flip(y, 2 if slot == 0 else near[k], 2)
        piece = s2.at[to, k, i] if h is None else s2.at[to, k, i, h]
        place = r2.at[k, slot, i] if h is None else r2.at[k, slot, i, h]
        y_first.setdefault((k, slot, i), []).append(remote(piece, place, y_peer[near[k] - 1]))

    x_second = {}
    y_second = {}

    def pass_x(i):
        for k in range(2):
            to = flip(x, near[1 - k], 2)
            x_first[k, 0, i].wait_recv()
            s1[to, k, i] = (s1[to, k, i].astype(F32) + r1[k, 0, i].astype(F32)).astype(BF)
            x_second[k, i] = remote(s1.at[to, k, i], r1.at[k, 2, i], x_peer[near[1 - k] - 1])

    def pass_y(i):
        for k in range(2):
            to = flip(y, near[1 - k], 2)
            for copy in y_first[k, 0, i]:
                copy.wait_recv()
            s2[to, k, i] = (s2[to, k, i].astype(F32) + r2[k, 0, i].astype(F32)).astype(BF)
            y_second[k, i] = remote(s2.at[to, k, i], r2.at[k, 2, i], y_peer[near[1 - k] - 1])

    gradient(1 - xh, 0, 0, store_x)
    send_x(1, 0, 0)
    send_x(0, 0, 0)
    send_x(1, 1, 0)
    gradient(0, 1, 0, store_y)
    send_y(0, 0, 0, 0)
    send_y(1, 0, 0, 0)
    gradient(1, 1, 0, store_y)
    send_y(0, 0, 0, 1)
    send_y(1, 0, 0, 1)
    send_y(0, 1, 0)
    send_y(1, 1, 0)
    gradient(xh, 0, 0, store_x)
    send_x(0, 1, 0)
    for copy in pair_a[2:]:
        copy.wait_recv()
    gradient(1 - xh, 0, 1, store_x)
    send_x(1, 0, 1)
    send_x(0, 0, 1)
    pass_on(1)
    pass_x(0)
    send_x(1, 1, 1)
    gradient(0, 1, 1, store_y)
    gradient(1, 1, 1, store_y)
    send_y(0, 0, 1)
    send_y(1, 0, 1)
    pass_y(0)
    send_y(0, 1, 1)
    send_y(1, 1, 1)
    gradient(xh, 0, 1, store_x)
    send_x(0, 1, 1)

    pair_w.wait_recv()

    @pl.loop(0, GROUPS)
    def _(i):
        att[i] = dot(probs_s[i].astype(BF), values_s[i], TN).astype(BF)

    def project(b):
        @pl.loop(0, 2)
        def _(j):
            cols = pl.ds(pl.multiple_of(j * 512, 512), 512)
            out_cols = pl.ds(pl.multiple_of(b * WIDTH + j * 512, 512), 512)
            total = dot(att[0], w_all[b, 0:GW, cols], NN)
            for i in range(1, GROUPS):
                total = total + dot(att[i], w_all[b, i * GW : (i + 1) * GW, cols], NN)
            out_stage[:, out_cols] = total.astype(BF)

    @pl.loop(0, 2)
    def _(j):
        rows = pl.ds(pl.multiple_of(j * 512, 512), 512)
        ag32[j] += dot(g_own[pair_block], w_all[pair_block, rows, :], NT)

    project(block)
    pass_x(1)
    pass_y(1)

    y2_moves = {}
    x2_moves = {}

    def second_y(i):
        for k in range(2):
            x_first[k, 1, i].wait_recv()
            x_second[k, i].wait_recv()
        y2_moves[i] = []
        for m in (2, 1, 3, 0):
            to = flip(y, m, 2)
            for k in range(2):
                total = s1[x, k, i, :, to].astype(F32)
                for j in (1, 2):
                    total = total + r1[k, j, i, :, to].astype(F32)
                t1[i, to, :, :, k * 256 : k * 256 + 256] = total.astype(BF)
            if m:
                y2_moves[i].append(remote(t1.at[i, to], p1.at[i, m - 1], y_peer[m - 1]))

    def second_x(i):
        for k in range(2):
            for copy in y_first[k, 1, i]:
                copy.wait_recv()
            y_second[k, i].wait_recv()
        x2_moves[i] = []
        for m in (2, 1, 3, 0):
            to = flip(x, m, 2)
            h = flip(xh, m // 2, 1)
            low_x = flip(xl, m % 2, 1)
            for k in range(2):
                total = s2[y, k, i, h, :, low_x].astype(F32)
                for j in (1, 2):
                    total = total + r2[k, j, i, h, :, low_x].astype(F32)
                t2[i, to, :, :, k * 256 : k * 256 + 256] = total.astype(BF)
            if m:
                x2_moves[i].append(remote(t2.at[i, to], p2.at[i, m - 1], x_peer[m - 1]))

    z_base = counter[0]
    counter[0] += 14

    def z_move(part, m):
        index = z_base + part * 7 + m - 1
        return pltpu.make_async_remote_copy(
            src_ref=u.at[part, flip(z, m, 3)],
            dst_ref=v.at[part, m - 1],
            send_sem=sem_s.at[index],
            recv_sem=sem_r.at[index],
            device_id=z_peer[m - 1],
            device_id_type=MESH,
        )

    def third(part, i):
        moves, mine, pieces = (y2_moves[i], t1[i, y], p1) if part == 0 else (x2_moves[i], t2[i, x], p2)
        for copy in moves:
            copy.wait_recv()
        total = mine.astype(F32)
        for m in range(3):
            total = total + pieces[i, m].astype(F32)
        u[part, 4 * i : 4 * i + 4] = total.astype(BF)
        for m in (4, 3, 5, 2, 6, 1, 7):

            @pl.when(flip(z, m, 3) // 4 == i)
            def _():
                z_move(part, m).start()

    second_y(0)
    second_x(0)
    project(pair_block)
    hand_over(0)
    hand_over(1)
    third(0, 0)
    second_y(1)
    third(1, 0)
    second_x(1)

    for half in range(2):
        for k in range(4, 8):
            far_moves[half][k].wait_recv()

    @pl.loop(0, 2)
    def _(j):
        rows = pl.ds(pl.multiple_of(j * 512, 512), 512)
        total = ag32[j] + dot(g_own[far_block], w_all[far_block, rows, :], NT)
        total = total + dot(g_own[far_pair_block], w_all[far_pair_block, rows, :], NT)
        low = total.astype(BF)
        ag[2 * j] = low[:, :GW]
        ag[2 * j + 1] = low[:, GW:]

    third(0, 1)
    third(1, 1)

    @pl.loop(0, GROUPS)
    def _(i):
        keys = keys_s[i]
        values = values_s[i]
        grads = ag[i]
        probs = probs_s[i]
        low = probs.astype(BF)
        sl = pl.ds(pl.multiple_of(i * GW, GW), GW)
        vp[:, sl] = gather_heads(dot(low, grads, NN))
        shaped = probs.reshape(GH, NEAR, TOK)
        prob_grad = dot(values, grads, NT).reshape(GH, NEAR, TOK)
        row_dot = jnp.sum(shaped * prob_grad, axis=1, keepdims=True)
        score_grad = (shaped * (prob_grad - row_dot)).reshape(GH * NEAR, TOK).astype(BF)
        turned_keys = dot(keys, turn, NN).astype(BF)
        part = SCALE * dot(score_grad, keys, TN)
        part_turned = SCALE * dot(score_grad, turned_keys, TN)
        qgrad[:, sl] = (part * cos_q() - part_turned * sin_q()).astype(BF)
        kp[:, sl] = gather_heads(SCALE * dot(score_grad, q_rot[i], NN))

    halo_out[0, 0:SPAN] = kp[2 * SPAN :, :]
    halo_out[0, SPAN:] = vp[2 * SPAN :, :]
    halo_out[1, 0:SPAN] = kp[0:SPAN, :]
    halo_out[1, SPAN:] = vp[0:SPAN, :]
    back = [
        remote(halo_out.at[0], halo_in.at[0], after),
        remote(halo_out.at[1], halo_in.at[1], before),
    ]

    project(far_block)
    project(far_pair_block)

    for copy in back:
        copy.wait_recv()
    vgrad_ref[...] = vp[SPAN : 2 * SPAN, :] + halo_in[0, SPAN:] + halo_in[1, SPAN:]
    key_total = kp[SPAN : 2 * SPAN, :] + halo_in[0, 0:SPAN] + halo_in[1, 0:SPAN]
    kgrad_ref[...] = key_total * cos_k - turned(key_total) * sin_k

    for part in range(2):
        for m in range(1, 8):
            z_move(part, m).wait_recv()
    for part in range(2):
        total = u[part, z].astype(F32)
        for m in range(7):
            total = total + v[part, m].astype(F32)
        wgrad_ref[:, part * 512 : part * 512 + 512] = total * factor

    for copy in started:
        copy.wait_send()
    for part in range(2):
        for m in range(1, 8):
            z_move(part, m).wait_send()


def finish(*refs):
    sems = refs[10]
    copies = [pltpu.make_async_copy(refs[i], refs[5 + i], sems.at[i]) for i in range(5)]
    for copy in copies:
        copy.start()
    for copy in copies:
        copy.wait()


def local(video_query, audio_key, audio_value, out_weight, grad_out, query_time, window):
    freqs = np.tile((10000.0 ** (-np.arange(HALF) / HALF)).astype(np.float32), 128 // HALF)
    factor = 1.0 / math.sqrt(TOK * lax.axis_size("ctx") * lax.axis_size("fsdp"))

    vmem = pl.BlockSpec(memory_space=pltpu.VMEM)
    hbm = pl.BlockSpec(memory_space=pltpu.HBM)
    n_sems = 88
    results = [
        ((TOK, 4 * WIDTH), BF),
        ((TOK, WIDTH), BF),
        ((SPAN, WIDTH), F32),
        ((SPAN, WIDTH), F32),
        ((16, WIDTH), F32),
    ]

    inputs = (
        video_query[0],
        audio_key[0],
        audio_value[0],
        out_weight,
        grad_out[0],
        query_time.reshape(1, TOK),
        window,
        jnp.asarray(freqs).reshape(1, 128),
    )

    def body(*refs):
        kernel(factor, *refs)

    outs = pl.pallas_call(
        body,
        name="fused",
        out_shape=[pltpu.VMEM(shape, dtype) for shape, dtype in results],
        in_specs=[hbm] * 8,
        out_specs=[vmem] * 5,
        scratch_shapes=[
            pltpu.VMEM((SPAN, WIDTH), BF),
            pltpu.VMEM((SPAN, WIDTH), BF),
            pltpu.VMEM((1, TOK), jnp.int32),
            pltpu.VMEM((2, TOK), jnp.int32),
            pltpu.VMEM((1, 128), F32),
            pltpu.VMEM((GROUPS, TOK, GW), BF),
            pltpu.VMEM((GROUPS, TOK, GW), BF),
            pltpu.VMEM((3, 2 * SPAN, WIDTH), BF),
            pltpu.VMEM((4, WIDTH, WIDTH), BF),
            pltpu.VMEM((4, TOK, WIDTH), BF),
            pltpu.VMEM((2, TOK, WIDTH), BF),
            pltpu.VMEM((GROUPS, GH * NEAR, GW), BF),
            pltpu.VMEM((GROUPS, GH * NEAR, GW), BF),
            pltpu.VMEM((GROUPS, GH * NEAR, TOK), F32),
            pltpu.VMEM((GROUPS, TOK, GW), BF),
            pltpu.VMEM((WIDTH, TOK), BF),
            pltpu.VMEM((WIDTH, TOK), BF),
            pltpu.VMEM((2, TOK, 512), F32),
            pltpu.VMEM((GROUPS, TOK, GW), BF),
            pltpu.VMEM((TOK, 256), F32),
            pltpu.VMEM((NEAR, WIDTH), F32),
            pltpu.VMEM((NEAR, WIDTH), F32),
            pltpu.VMEM((2, 2 * SPAN, WIDTH), F32),
            pltpu.VMEM((2, 2 * SPAN, WIDTH), F32),
            pltpu.VMEM((4, 2, 2, 4, 4, 16, 256), BF),
            pltpu.VMEM((2, 3, 2, 4, 4, 16, 256), BF),
            pltpu.VMEM((4, 2, 2, 2, 4, 2, 16, 256), BF),
            pltpu.VMEM((2, 3, 2, 2, 4, 2, 16, 256), BF),
            pltpu.VMEM((2, 4, 4, 16, 512), BF),
            pltpu.VMEM((2, 3, 4, 16, 512), BF),
            pltpu.VMEM((2, 4, 4, 16, 512), BF),
            pltpu.VMEM((2, 3, 4, 16, 512), BF),
            pltpu.VMEM((2, 8, 16, 512), BF),
            pltpu.VMEM((2, 7, 16, 512), BF),
            pltpu.SemaphoreType.DMA((24,)),
            pltpu.SemaphoreType.DMA((n_sems,)),
            pltpu.SemaphoreType.DMA((n_sems,)),
        ],
        compiler_params=pltpu.CompilerParams(
            collective_id=0, has_side_effects=True, vmem_limit_bytes=46 << 20
        ),
    )(
        *[pltpu.with_memory_space_constraint(arg, pltpu.HBM) for arg in inputs]
    )
    outs = pl.pallas_call(
        finish,
        name="finish",
        out_shape=[jax.ShapeDtypeStruct(shape, dtype) for shape, dtype in results],
        in_specs=[vmem] * 5,
        out_specs=[hbm] * 5,
        scratch_shapes=[pltpu.SemaphoreType.DMA((5,))],
        compiler_params=pltpu.CompilerParams(vmem_limit_bytes=4 << 20),
    )(*[pltpu.with_memory_space_constraint(out, pltpu.VMEM) for out in outs])
    output, query_grad, key_grad, value_grad, weight_grad = outs
    return (output[None], query_grad[None], key_grad[None], value_grad[None], weight_grad)


def solution(mesh):
    in_specs = (
        P("fsdp", "ctx", None),
        P("fsdp", "ctx", None),
        P("fsdp", "ctx", None),
        P(None, "fsdp"),
        P("fsdp", "ctx", None),
        P("ctx"),
        P(None, "ctx"),
    )
    out_specs = (
        P("fsdp", "ctx", None),
        P("fsdp", "ctx", None),
        P("fsdp", "ctx", None),
        P("fsdp", "ctx", None),
        P("ctx", "fsdp"),
    )
    return jax.shard_map(local, mesh=mesh, in_specs=in_specs, out_specs=out_specs, check_vma=False)
```

```python
import math

import jax
import jax.numpy as jnp
import numpy as np
from jax import lax
from jax.experimental import pallas as pl
from jax.experimental.pallas import tpu as pltpu
from jax.sharding import PartitionSpec as P

DH = 64
HALF = DH // 2
TOK = 512
WIDTH = 1024
SPAN = 8
NEAR = 3 * SPAN
GROUPS = 4
GW = WIDTH // GROUPS
GH = GW // DH
WIDE = 384
SCALE = 1.0 / math.sqrt(DH)
MESH = pl.DeviceIdType.MESH
BF = jnp.bfloat16
F32 = jnp.float32

NN = (((1,), (0,)), ((), ()))
NT = (((1,), (1,)), ((), ()))
TN = (((0,), (0,)), ((), ()))


def dot(a, b, dims):
    return lax.dot_general(a, b, dims, preferred_element_type=F32)


def flip(value, mask, bits):
    out = 0
    for bit in range(bits):
        digit = (value // (1 << bit)) % 2
        if (mask >> bit) & 1:
            digit = 1 - digit
        out = out + digit * (1 << bit)
    return out


def kernel(
    factor,
    query_hbm,
    key_hbm,
    value_hbm,
    weight_hbm,
    grad_hbm,
    time_hbm,
    window_hbm,
    out_stage,
    qgrad,
    kgrad_ref,
    vgrad_ref,
    wgrad_ref,
    key_ref,
    value_ref,
    time_ref,
    window_ref,
    q_raw,
    q_rot,
    near_kv,
    w_all,
    g_own,
    g_pair,
    keys_s,
    values_s,
    probs_s,
    att,
    att_t,
    att_t_pair,
    ag32,
    ag,
    table,
    kp,
    vp,
    halo_out,
    halo_in,
    s1a,
    s1b,
    r1a,
    r1b,
    s2,
    r2,
    t1,
    p1,
    t2,
    p2,
    u,
    v,
    loc,
    sem_s,
    sem_r,
):
    ctx = lax.axis_index("ctx")
    fs = lax.axis_index("fsdp")
    z = ctx // 8
    y = (ctx // 2) % 4
    xl = ctx % 2
    xh = fs // 2
    core = fs % 2
    x = xh * 2 + xl
    n_ctx = 64

    def device(x_, y_, z_, core_):
        return (z_ * 8 + y_ * 2 + x_ % 2, (x_ // 2) * 2 + core_)

    pair = (ctx, xh * 2 + 1 - core)
    after = ((ctx + 1) % n_ctx, fs)
    before = ((ctx + n_ctx - 1) % n_ctx, fs)
    x_peer = [device(flip(x, m, 2), y, z, core) for m in (1, 2, 3)]
    y_peer = [device(x, flip(y, m, 2), z, core) for m in (1, 2, 3)]
    z_peer = [device(x, y, flip(z, m, 3), core) for m in range(1, 8)]
    z_step = {d: device(x, y, (z + d + 8) % 8, core) for d in (1, -1, 2, -2)}
    y_step = {d: device(x, (y + d + 4) % 4, z, core) for d in (1, -1)}

    counter = [0]

    def remote(src, dst, target):
        index = counter[0]
        counter[0] += 1
        copy = pltpu.make_async_remote_copy(
            src_ref=src,
            dst_ref=dst,
            send_sem=sem_s.at[index],
            recv_sem=sem_r.at[index],
            device_id=target,
            device_id_type=MESH,
        )
        copy.start()
        started.append(copy)
        return copy

    started = []
    local_counter = [0]

    def local(src, dst):
        index = local_counter[0]
        local_counter[0] += 1
        copy = pltpu.make_async_copy(src, dst, loc.at[index])
        copy.start()
        return copy

    block = fs
    pair_block = xh * 2 + 1 - core
    far_block = (1 - xh) * 2 + core
    far_pair_block = (1 - xh) * 2 + 1 - core
    small = [
        local(key_hbm, key_ref),
        local(value_hbm, value_ref),
        local(time_hbm, time_ref),
        local(window_hbm, window_ref),
    ]

    barrier = pltpu.get_barrier_semaphore()
    greet = [pair, after, before] + x_peer + y_peer + z_peer
    for target in greet:
        pl.semaphore_signal(barrier, inc=1, device_id=target, device_id_type=MESH)

    load_q = [local(query_hbm.at[:, pl.ds(i * GW, GW)], q_raw.at[i]) for i in range(GROUPS)]
    load_g = [local(grad_hbm.at[:, pl.ds(i * WIDTH, WIDTH)], g_own.at[i]) for i in range(4)]
    load_w = local(weight_hbm, w_all.at[block])

    lane = lax.broadcasted_iota(jnp.int32, (SPAN, WIDTH), 1) % DH

    def turned(values):
        left = pltpu.roll(values, WIDTH - HALF, 1)
        right = pltpu.roll(values, HALF, 1)
        return jnp.where(lane < HALF, -left, right)

    freqs = jnp.zeros((1, 128), F32)
    frequency = lax.broadcasted_iota(jnp.int32, (1, 128), 1) % HALF
    for m in range(HALF):
        freqs = jnp.where(frequency == m, np.float32(10000.0 ** (-m / HALF)), freqs)
    own_row = lax.broadcasted_iota(jnp.int32, (SPAN, 1), 0) + ctx * SPAN
    own_angles = own_row.astype(F32) * freqs
    cos_k = jnp.concatenate([jnp.cos(own_angles)] * (WIDTH // 128), axis=1)
    sin_k = jnp.concatenate([jnp.sin(own_angles)] * (WIDTH // 128), axis=1)
    for copy in small:
        copy.wait()
    raw_k = key_ref[...].astype(F32)
    near_kv[0] = jnp.concatenate(
        [raw_k * cos_k + turned(raw_k) * sin_k, value_ref[...].astype(F32)], axis=0
    ).astype(BF)

    pl.semaphore_wait(barrier, len(greet))

    halo_a = remote(near_kv.at[0], near_kv.at[1], after)
    halo_b = remote(near_kv.at[0], near_kv.at[2], before)
    quarter = (z + 2 * (y % 2)) % 4
    cross = []
    for half in range(2):
        rows = pl.ds(quarter * 256 + half * 128, 128)
        cross.append(remote(weight_hbm.at[rows], w_all.at[block, rows], x_peer[2]))
    pair_g = [
        remote(
            grad_hbm.at[:, pl.ds(pl.multiple_of((2 * h + 1 - core) * WIDTH, WIDTH), WIDTH)],
            g_pair.at[h],
            pair,
        )
        for h in range(2)
    ]

    near_row = lax.broadcasted_iota(jnp.int32, (32, 1), 0) + ctx * SPAN - SPAN
    angles = near_row.astype(F32) * freqs
    near_table = jnp.concatenate([jnp.cos(angles), jnp.sin(angles)], axis=1)
    pieces = []
    rest = near_table
    for _ in range(3):
        piece = rest.astype(BF).astype(F32)
        pieces.append(piece)
        rest = rest - piece
    time_row = jnp.where(near_row == time_ref[...], 1.0, 0.0)
    chosen = jnp.concatenate([time_row] * 3, axis=0).astype(BF)
    table[...] = dot(chosen, jnp.concatenate(pieces, axis=0).astype(BF), TN)

    def cos_q():
        return jnp.concatenate([table[:, :128]] * 2, axis=1)

    def sin_q():
        return jnp.concatenate([table[:, 128:]] * 2, axis=1)

    lane_i = lax.broadcasted_iota(jnp.int32, (GW, GW), 0)
    lane_j = lax.broadcasted_iota(jnp.int32, (GW, GW), 1)
    first_j = lane_j % DH < HALF
    turn = jnp.where(
        first_j & (lane_i == lane_j + HALF),
        -1.0,
        jnp.where((~first_j) & (lane_i == lane_j - HALF), 1.0, 0.0),
    ).astype(BF)
    for copy in load_q:
        copy.wait()

    @pl.loop(0, GROUPS)
    def _(i):
        raw = q_raw[i]
        q_rot[i] = (raw.astype(F32) * cos_q() + dot(raw, turn, NN) * sin_q()).astype(BF)

    def early(j):
        rows = pl.ds(j * 512, 512)
        ag32[j] = dot(g_own[block], w_all[block, rows, :], NT)

    for copy in load_g:
        copy.wait()
    load_w.wait()
    early(0)

    halo_a.wait_recv()
    halo_b.wait_recv()

    near_index = (
        lax.broadcasted_iota(jnp.int32, (NEAR, TOK), 0) + ctx * SPAN - SPAN
    )
    allowed = (near_index >= window_ref[0:1, :]) & (near_index < window_ref[1:2, :])
    head_row = lax.broadcasted_iota(jnp.int32, (GH, NEAR, GW), 0)
    head_col = lax.broadcasted_iota(jnp.int32, (GH, NEAR, GW), 2) // DH
    own_head = head_row == head_col

    def spread(row, i):
        sl = pl.ds(pl.multiple_of(i * GW, GW), GW)
        parts = [near_kv[slot, :, sl].astype(F32)[row : row + SPAN] for slot in (1, 0, 2)]
        near = jnp.concatenate(parts, axis=0)
        wide = jnp.where(own_head, near[None], 0.0)
        return wide.reshape(GH * NEAR, GW).astype(BF)

    def gather_heads(wide):
        shaped = wide.reshape(GH, NEAR, GW)
        return jnp.sum(jnp.where(own_head, shaped, 0.0), axis=0)

    pair_a = []
    for i in range(GROUPS):
        keys = spread(0, i)
        values = spread(SPAN, i)
        keys_s[i] = keys
        values_s[i] = values
        scores = SCALE * dot(keys, q_rot[i], NT).reshape(GH, NEAR, TOK)
        masked = jnp.where(allowed[None], scores, -1e30)
        highest = jnp.max(masked, axis=1, keepdims=True)
        expo = jnp.where(allowed[None], jnp.exp(masked - highest), 0.0)
        probs = (expo / jnp.sum(expo, axis=1, keepdims=True)).reshape(GH * NEAR, TOK)
        probs_s[i] = probs
        low = probs.astype(BF)
        rows = pl.ds(i * GW, GW)
        att_t[rows, :] = dot(values, low, TN).astype(BF)
        pair_a.append(remote(att_t.at[rows], att_t_pair.at[rows], pair))

    pair_w = remote(weight_hbm, w_all.at[block], pair)
    early(1)

    far_moves = []

    def pass_on(half):
        cross[half].wait_recv()
        start = quarter * 256 + half * 128
        piece = w_all.at[far_block, pl.ds(start, 128)]
        one = w_all.at[far_block, pl.ds(start, 64)]
        two = w_all.at[far_block, pl.ds(start + 64, 64)]
        up, down = (y_step[1], y_step[-1]) if half == 0 else (z_step[2], z_step[-2])
        moves = [
            remote(piece, piece, z_step[1]),
            remote(piece, piece, z_step[-1]),
            remote(one, one, up),
            remote(two, two, down),
            remote(piece, piece, pair),
        ]
        far_moves.append(moves)

    def hand_over(half):
        for k, step in ((0, 3), (1, 1), (2, 2)):
            far_moves[half][k].wait_recv()
            if k == 2:
                far_moves[half][3].wait_recv()
            rows = pl.ds(((quarter + step) % 4) * 256 + half * 128, 128)
            piece = w_all.at[far_block, rows]
            far_moves[half].append(remote(piece, piece, pair))

    pass_on(0)

    for copy in pair_g + pair_a[:2]:
        copy.wait_recv()

    def gradient(h, part, i, store):
        cols = slice(part * 512, (part + 1) * 512)
        rows = slice(i * 512, (i + 1) * 512)
        total = dot(att_t[rows, :], g_own[2 * h + core, :, cols], NN)
        total = total + dot(att_t_pair[rows, :], g_pair[h, :, cols], NN)
        store(h, i, total.astype(BF).reshape(4, 4, 2, 16, 512))

    s1, r1 = (s1a, s1b), (r1a, r1b)
    x_cols = (slice(0, WIDE), slice(WIDE, 512))

    def store_x(h, i, total):
        for low_x in range(2):
            for k in range(2):
                s1[k][2 * h + low_x, i] = total[:, :, low_x, :, x_cols[k]]

    def store_y(h, i, total):
        for to_y in range(4):
            for k in range(2):
                s2[to_y, k, i, h] = total[:, to_y, :, :, k * 256 : k * 256 + 256]

    near = (1, 3)
    x_first = {}
    y_first = {}

    def send_x(k, slot, i):
        to = flip(x, 2 if slot == 0 else near[k], 2)
        x_first[k, slot, i] = remote(s1[k].at[to, i], r1[k].at[slot, i], x_peer[near[k] - 1])

    def send_y(k, slot, i, h=None):
        to = flip(y, 2 if slot == 0 else near[k], 2)
        piece = s2.at[to, k, i] if h is None else s2.at[to, k, i, h]
        place = r2.at[k, slot, i] if h is None else r2.at[k, slot, i, h]
        y_first.setdefault((k, slot, i), []).append(remote(piece, place, y_peer[near[k] - 1]))

    x_second = {}
    y_second = {}

    def pass_x(i):
        for k in range(2):
            to = flip(x, near[1 - k], 2)
            x_first[k, 0, i].wait_recv()
            s1[k][to, i] = (s1[k][to, i].astype(F32) + r1[k][0, i].astype(F32)).astype(BF)
            x_second[k, i] = remote(s1[k].at[to, i], r1[k].at[2, i], x_peer[near[1 - k] - 1])

    def pass_y(i):
        for k in range(2):
            to = flip(y, near[1 - k], 2)
            for copy in y_first[k, 0, i]:
                copy.wait_recv()
            s2[to, k, i] = (s2[to, k, i].astype(F32) + r2[k, 0, i].astype(F32)).astype(BF)
            y_second[k, i] = remote(s2.at[to, k, i], r2.at[k, 2, i], y_peer[near[1 - k] - 1])

    gradient(0, 1, 0, store_y)
    send_y(0, 0, 0, 0)
    send_y(1, 0, 0, 0)
    gradient(1 - xh, 0, 0, store_x)
    send_x(0, 0, 0)
    send_x(1, 0, 0)
    send_x(1, 1, 0)
    gradient(1, 1, 0, store_y)
    send_y(0, 0, 0, 1)
    send_y(1, 0, 0, 1)
    send_y(0, 1, 0)
    send_y(1, 1, 0)
    gradient(xh, 0, 0, store_x)
    send_x(0, 1, 0)
    for copy in pair_a[2:]:
        copy.wait_recv()
    gradient(1 - xh, 0, 1, store_x)
    send_x(1, 0, 1)
    send_x(0, 0, 1)
    gradient(0, 1, 1, store_y)
    gradient(1, 1, 1, store_y)
    send_y(0, 0, 1)
    send_y(1, 0, 1)
    pass_on(1)
    gradient(xh, 0, 1, store_x)
    pass_x(0)
    send_x(1, 1, 1)
    send_x(0, 1, 1)
    pass_y(0)
    send_y(0, 1, 1)
    send_y(1, 1, 1)

    pair_w.wait_recv()

    @pl.loop(0, GROUPS)
    def _(i):
        att[i] = dot(probs_s[i].astype(BF), values_s[i], TN).astype(BF)

    def project(b):
        @pl.loop(0, 2)
        def _(j):
            cols = pl.ds(pl.multiple_of(j * 512, 512), 512)
            out_cols = pl.ds(pl.multiple_of(b * WIDTH + j * 512, 512), 512)
            total = dot(att[0], w_all[b, 0:GW, cols], NN)
            for i in range(1, GROUPS):
                total = total + dot(att[i], w_all[b, i * GW : (i + 1) * GW, cols], NN)
            out_stage[:, out_cols] = total.astype(BF)

    @pl.loop(0, 2)
    def _(j):
        rows = pl.ds(pl.multiple_of(j * 512, 512), 512)
        ag32[j] += dot(g_own[pair_block], w_all[pair_block, rows, :], NT)

    project(block)
    pass_x(1)
    pass_y(1)

    y2_moves = {}
    x2_moves = {}

    def second_y(i):
        for k in range(2):
            x_first[k, 1, i].wait_recv()
            x_second[k, i].wait_recv()
        y2_moves[i] = []
        for m in (2, 1, 3, 0):
            to = flip(y, m, 2)
            for k in range(2):
                total = s1[k][x, i, :, to].astype(F32)
                for j in (1, 2):
                    total = total + r1[k][j, i, :, to].astype(F32)
                t1[i, to, :, :, x_cols[k]] = total.astype(BF)
            if m:
                y2_moves[i].append(remote(t1.at[i, to], p1.at[i, m - 1], y_peer[m - 1]))

    def second_x(i):
        for k in range(2):
            for copy in y_first[k, 1, i]:
                copy.wait_recv()
            y_second[k, i].wait_recv()
        x2_moves[i] = []
        for m in (2, 1, 3, 0):
            to = flip(x, m, 2)
            h = flip(xh, m // 2, 1)
            low_x = flip(xl, m % 2, 1)
            for k in range(2):
                total = s2[y, k, i, h, :, low_x].astype(F32)
                for j in (1, 2):
                    total = total + r2[k, j, i, h, :, low_x].astype(F32)
                t2[i, to, :, :, k * 256 : k * 256 + 256] = total.astype(BF)
            if m:
                x2_moves[i].append(remote(t2.at[i, to], p2.at[i, m - 1], x_peer[m - 1]))

    z_base = counter[0]
    counter[0] += 14

    def z_move(part, m):
        index = z_base + part * 7 + m - 1
        return pltpu.make_async_remote_copy(
            src_ref=u.at[part, flip(z, m, 3)],
            dst_ref=v.at[part, m - 1],
            send_sem=sem_s.at[index],
            recv_sem=sem_r.at[index],
            device_id=z_peer[m - 1],
            device_id_type=MESH,
        )

    def third(part, i):
        moves, mine, pieces = (y2_moves[i], t1[i, y], p1) if part == 0 else (x2_moves[i], t2[i, x], p2)
        for copy in moves:
            copy.wait_recv()
        total = mine.astype(F32)
        for m in range(3):
            total = total + pieces[i, m].astype(F32)
        u[part, 4 * i : 4 * i + 4] = total.astype(BF)
        for m in (4, 3, 5, 2, 6, 1, 7):

            @pl.when(flip(z, m, 3) // 4 == i)
            def _():
                z_move(part, m).start()

    second_y(0)
    second_x(0)
    project(pair_block)
    hand_over(0)
    hand_over(1)
    third(0, 0)
    second_y(1)
    third(1, 0)
    second_x(1)

    for half in range(2):
        for k in range(4, 8):
            far_moves[half][k].wait_recv()

    @pl.loop(0, 2)
    def _(j):
        rows = pl.ds(pl.multiple_of(j * 512, 512), 512)
        total = ag32[j] + dot(g_own[far_block], w_all[far_block, rows, :], NT)
        total = total + dot(g_own[far_pair_block], w_all[far_pair_block, rows, :], NT)
        low = total.astype(BF)
        ag[2 * j] = low[:, :GW]
        ag[2 * j + 1] = low[:, GW:]

    third(0, 1)
    third(1, 1)

    @pl.loop(0, GROUPS)
    def _(i):
        keys = keys_s[i]
        values = values_s[i]
        grads = ag[i]
        probs = probs_s[i]
        low = probs.astype(BF)
        sl = pl.ds(pl.multiple_of(i * GW, GW), GW)
        vp[:, sl] = gather_heads(dot(low, grads, NN))
        shaped = probs.reshape(GH, NEAR, TOK)
        prob_grad = dot(values, grads, NT).reshape(GH, NEAR, TOK)
        row_dot = jnp.sum(shaped * prob_grad, axis=1, keepdims=True)
        score_grad = (shaped * (prob_grad - row_dot)).reshape(GH * NEAR, TOK).astype(BF)
        turned_keys = dot(keys, turn, NN).astype(BF)
        part = SCALE * dot(score_grad, keys, TN)
        part_turned = SCALE * dot(score_grad, turned_keys, TN)
        qgrad[:, sl] = (part * cos_q() - part_turned * sin_q()).astype(BF)
        kp[:, sl] = gather_heads(SCALE * dot(score_grad, q_rot[i], NN))

    halo_out[0, 0:SPAN] = kp[2 * SPAN :, :]
    halo_out[0, SPAN:] = vp[2 * SPAN :, :]
    halo_out[1, 0:SPAN] = kp[0:SPAN, :]
    halo_out[1, SPAN:] = vp[0:SPAN, :]
    back = [
        remote(halo_out.at[0], halo_in.at[0], after),
        remote(halo_out.at[1], halo_in.at[1], before),
    ]

    project(far_block)
    project(far_pair_block)

    for copy in back:
        copy.wait_recv()
    vgrad_ref[...] = vp[SPAN : 2 * SPAN, :] + halo_in[0, SPAN:] + halo_in[1, SPAN:]
    key_total = kp[SPAN : 2 * SPAN, :] + halo_in[0, 0:SPAN] + halo_in[1, 0:SPAN]
    kgrad_ref[...] = key_total * cos_k - turned(key_total) * sin_k

    for part in range(2):
        for m in range(1, 8):
            z_move(part, m).wait_recv()
    for part in range(2):
        total = u[part, z].astype(F32)
        for m in range(7):
            total = total + v[part, m].astype(F32)
        wgrad_ref[:, part * 512 : part * 512 + 512] = total * factor

    for copy in started:
        copy.wait_send()
    for part in range(2):
        for m in range(1, 8):
            z_move(part, m).wait_send()


def finish(*refs):
    sems = refs[10]
    copies = [pltpu.make_async_copy(refs[i], refs[5 + i], sems.at[i]) for i in range(5)]
    for copy in copies:
        copy.start()
    for copy in copies:
        copy.wait()


def local(video_query, audio_key, audio_value, out_weight, grad_out, query_time, window):
    factor = 1.0 / math.sqrt(TOK * lax.axis_size("ctx") * lax.axis_size("fsdp"))

    vmem = pl.BlockSpec(memory_space=pltpu.VMEM)
    hbm = pl.BlockSpec(memory_space=pltpu.HBM)
    n_sems = 88
    results = [
        ((TOK, 4 * WIDTH), BF),
        ((TOK, WIDTH), BF),
        ((SPAN, WIDTH), F32),
        ((SPAN, WIDTH), F32),
        ((16, WIDTH), F32),
    ]

    inputs = (
        video_query[0],
        audio_key[0],
        audio_value[0],
        out_weight,
        grad_out[0],
        query_time.reshape(1, TOK),
        window,
    )

    def body(*refs):
        kernel(factor, *refs)

    outs = pl.pallas_call(
        body,
        name="fused",
        out_shape=[pltpu.VMEM(shape, dtype) for shape, dtype in results],
        in_specs=[hbm] * 7,
        out_specs=[vmem] * 5,
        scratch_shapes=[
            pltpu.VMEM((SPAN, WIDTH), BF),
            pltpu.VMEM((SPAN, WIDTH), BF),
            pltpu.VMEM((1, TOK), jnp.int32),
            pltpu.VMEM((2, TOK), jnp.int32),
            pltpu.VMEM((GROUPS, TOK, GW), BF),
            pltpu.VMEM((GROUPS, TOK, GW), BF),
            pltpu.VMEM((3, 2 * SPAN, WIDTH), BF),
            pltpu.VMEM((4, WIDTH, WIDTH), BF),
            pltpu.VMEM((4, TOK, WIDTH), BF),
            pltpu.VMEM((2, TOK, WIDTH), BF),
            pltpu.VMEM((GROUPS, GH * NEAR, GW), BF),
            pltpu.VMEM((GROUPS, GH * NEAR, GW), BF),
            pltpu.VMEM((GROUPS, GH * NEAR, TOK), F32),
            pltpu.VMEM((GROUPS, TOK, GW), BF),
            pltpu.VMEM((WIDTH, TOK), BF),
            pltpu.VMEM((WIDTH, TOK), BF),
            pltpu.VMEM((2, TOK, 512), F32),
            pltpu.VMEM((GROUPS, TOK, GW), BF),
            pltpu.VMEM((TOK, 256), F32),
            pltpu.VMEM((NEAR, WIDTH), F32),
            pltpu.VMEM((NEAR, WIDTH), F32),
            pltpu.VMEM((2, 2 * SPAN, WIDTH), F32),
            pltpu.VMEM((2, 2 * SPAN, WIDTH), F32),
            pltpu.VMEM((4, 2, 4, 4, 16, WIDE), BF),
            pltpu.VMEM((4, 2, 4, 4, 16, 512 - WIDE), BF),
            pltpu.VMEM((3, 2, 4, 4, 16, WIDE), BF),
            pltpu.VMEM((3, 2, 4, 4, 16, 512 - WIDE), BF),
            pltpu.VMEM((4, 2, 2, 2, 4, 2, 16, 256), BF),
            pltpu.VMEM((2, 3, 2, 2, 4, 2, 16, 256), BF),
            pltpu.VMEM((2, 4, 4, 16, 512), BF),
            pltpu.VMEM((2, 3, 4, 16, 512), BF),
            pltpu.VMEM((2, 4, 4, 16, 512), BF),
            pltpu.VMEM((2, 3, 4, 16, 512), BF),
            pltpu.VMEM((2, 8, 16, 512), BF),
            pltpu.VMEM((2, 7, 16, 512), BF),
            pltpu.SemaphoreType.DMA((24,)),
            pltpu.SemaphoreType.DMA((n_sems,)),
            pltpu.SemaphoreType.DMA((n_sems,)),
        ],
        compiler_params=pltpu.CompilerParams(
            collective_id=0, has_side_effects=True, vmem_limit_bytes=46 << 20
        ),
    )(
        *[pltpu.with_memory_space_constraint(arg, pltpu.HBM) for arg in inputs]
    )
    outs = pl.pallas_call(
        finish,
        name="finish",
        out_shape=[jax.ShapeDtypeStruct(shape, dtype) for shape, dtype in results],
        in_specs=[vmem] * 5,
        out_specs=[hbm] * 5,
        scratch_shapes=[pltpu.SemaphoreType.DMA((5,))],
        compiler_params=pltpu.CompilerParams(vmem_limit_bytes=4 << 20),
    )(*[pltpu.with_memory_space_constraint(out, pltpu.VMEM) for out in outs])
    output, query_grad, key_grad, value_grad, weight_grad = outs
    return (output[None], query_grad[None], key_grad[None], value_grad[None], weight_grad)


def solution(mesh):
    in_specs = (
        P("fsdp", "ctx", None),
        P("fsdp", "ctx", None),
        P("fsdp", "ctx", None),
        P(None, "fsdp"),
        P("fsdp", "ctx", None),
        P("ctx"),
        P(None, "ctx"),
    )
    out_specs = (
        P("fsdp", "ctx", None),
        P("fsdp", "ctx", None),
        P("fsdp", "ctx", None),
        P("fsdp", "ctx", None),
        P("ctx", "fsdp"),
    )
    return jax.shard_map(local, mesh=mesh, in_specs=in_specs, out_specs=out_specs, check_vma=False)
```

```python
import math

import jax
import jax.numpy as jnp
import numpy as np
from jax import lax
from jax.experimental import pallas as pl
from jax.experimental.pallas import tpu as pltpu
from jax.sharding import PartitionSpec as P

DH = 64
HALF = DH // 2
TOK = 512
WIDTH = 1024
SPAN = 8
NEAR = 3 * SPAN
GROUPS = 4
GW = WIDTH // GROUPS
GH = GW // DH
WIDE = 384
SCALE = 1.0 / math.sqrt(DH)
MESH = pl.DeviceIdType.MESH
BF = jnp.bfloat16
F32 = jnp.float32

NN = (((1,), (0,)), ((), ()))
NT = (((1,), (1,)), ((), ()))
TN = (((0,), (0,)), ((), ()))


def dot(a, b, dims):
    return lax.dot_general(a, b, dims, preferred_element_type=F32)


def flip(value, mask, bits):
    out = 0
    for bit in range(bits):
        digit = (value // (1 << bit)) % 2
        if (mask >> bit) & 1:
            digit = 1 - digit
        out = out + digit * (1 << bit)
    return out


def kernel(
    factor,
    query_hbm,
    pair_hbm,
    weight_hbm,
    grad_hbm,
    time_hbm,
    window_hbm,
    out_stage,
    qgrad,
    kgrad_ref,
    vgrad_ref,
    wgrad_ref,
    pair_ref,
    time_ref,
    window_ref,
    q_raw,
    q_rot,
    near_kv,
    w_all,
    g_own,
    g_pair,
    keys_s,
    values_s,
    probs_s,
    att,
    att_t,
    att_t_pair,
    ag32,
    ag,
    table,
    kp,
    vp,
    halo_out,
    halo_in,
    s1a,
    s1b,
    r1a,
    r1b,
    s2,
    r2,
    t1,
    p1,
    t2,
    p2,
    u,
    v,
    loc,
    sem_s,
    sem_r,
):
    ctx = lax.axis_index("ctx")
    fs = lax.axis_index("fsdp")
    z = ctx // 8
    y = (ctx // 2) % 4
    xl = ctx % 2
    xh = fs // 2
    core = fs % 2
    x = xh * 2 + xl
    n_ctx = 64

    def device(x_, y_, z_, core_):
        return (z_ * 8 + y_ * 2 + x_ % 2, (x_ // 2) * 2 + core_)

    pair = (ctx, xh * 2 + 1 - core)
    after = ((ctx + 1) % n_ctx, fs)
    before = ((ctx + n_ctx - 1) % n_ctx, fs)
    x_peer = [device(flip(x, m, 2), y, z, core) for m in (1, 2, 3)]
    y_peer = [device(x, flip(y, m, 2), z, core) for m in (1, 2, 3)]
    z_peer = [device(x, y, flip(z, m, 3), core) for m in range(1, 8)]
    z_step = {d: device(x, y, (z + d + 8) % 8, core) for d in (1, -1, 2, -2)}
    y_step = {d: device(x, (y + d + 4) % 4, z, core) for d in (1, -1)}

    counter = [0]

    def remote(src, dst, target):
        index = counter[0]
        counter[0] += 1
        copy = pltpu.make_async_remote_copy(
            src_ref=src,
            dst_ref=dst,
            send_sem=sem_s.at[index],
            recv_sem=sem_r.at[index],
            device_id=target,
            device_id_type=MESH,
        )
        copy.start()
        started.append(copy)
        return copy

    started = []
    local_counter = [0]

    def local(src, dst):
        index = local_counter[0]
        local_counter[0] += 1
        copy = pltpu.make_async_copy(src, dst, loc.at[index])
        copy.start()
        return copy

    block = fs
    pair_block = xh * 2 + 1 - core
    far_block = (1 - xh) * 2 + core
    far_pair_block = (1 - xh) * 2 + 1 - core
    small = [
        local(pair_hbm, pair_ref),
        local(time_hbm, time_ref),
        local(window_hbm, window_ref),
    ]

    barrier = pltpu.get_barrier_semaphore()
    greet = [pair, after, before] + x_peer + y_peer + z_peer
    for target in greet:
        pl.semaphore_signal(barrier, inc=1, device_id=target, device_id_type=MESH)

    load_q = [local(query_hbm.at[:, pl.ds(i * GW, GW)], q_raw.at[i]) for i in range(GROUPS)]
    load_g = [local(grad_hbm.at[:, pl.ds(i * WIDTH, WIDTH)], g_own.at[i]) for i in range(4)]
    load_w = local(weight_hbm, w_all.at[block])

    lane = lax.broadcasted_iota(jnp.int32, (SPAN, WIDTH), 1) % DH

    def turned(values):
        left = pltpu.roll(values, WIDTH - HALF, 1)
        right = pltpu.roll(values, HALF, 1)
        return jnp.where(lane < HALF, -left, right)

    freqs = jnp.zeros((1, 128), F32)
    frequency = lax.broadcasted_iota(jnp.int32, (1, 128), 1) % HALF
    for m in range(HALF):
        freqs = jnp.where(frequency == m, np.float32(10000.0 ** (-m / HALF)), freqs)
    own_row = lax.broadcasted_iota(jnp.int32, (SPAN, 1), 0) + ctx * SPAN
    own_angles = own_row.astype(F32) * freqs
    cos_k = jnp.concatenate([jnp.cos(own_angles)] * (WIDTH // 128), axis=1)
    sin_k = jnp.concatenate([jnp.sin(own_angles)] * (WIDTH // 128), axis=1)
    for copy in small:
        copy.wait()
    own_pair = pair_ref[...].astype(F32)
    raw_k = own_pair[:SPAN]
    near_kv[0] = jnp.concatenate(
        [raw_k * cos_k + turned(raw_k) * sin_k, own_pair[SPAN:]], axis=0
    ).astype(BF)

    pl.semaphore_wait(barrier, len(greet))

    halo_a = remote(near_kv.at[0], near_kv.at[1], after)
    halo_b = remote(near_kv.at[0], near_kv.at[2], before)
    quarter = (z + 2 * (y % 2)) % 4
    cross = []
    for half in range(2):
        rows = pl.ds(quarter * 256 + half * 128, 128)
        cross.append(remote(weight_hbm.at[rows], w_all.at[block, rows], x_peer[2]))
    pair_g = [
        remote(
            grad_hbm.at[:, pl.ds(pl.multiple_of((2 * h + 1 - core) * WIDTH, WIDTH), WIDTH)],
            g_pair.at[h],
            pair,
        )
        for h in range(2)
    ]

    near_row = lax.broadcasted_iota(jnp.int32, (32, 1), 0) + ctx * SPAN - SPAN
    angles = near_row.astype(F32) * freqs
    near_table = jnp.concatenate([jnp.cos(angles), jnp.sin(angles)], axis=1)
    pieces = []
    rest = near_table
    for _ in range(3):
        piece = rest.astype(BF).astype(F32)
        pieces.append(piece)
        rest = rest - piece
    time_row = jnp.where(near_row == time_ref[...], 1.0, 0.0)
    chosen = jnp.concatenate([time_row] * 3, axis=0).astype(BF)
    table[...] = dot(chosen, jnp.concatenate(pieces, axis=0).astype(BF), TN)

    def cos_q():
        return jnp.concatenate([table[:, :128]] * 2, axis=1)

    def sin_q():
        return jnp.concatenate([table[:, 128:]] * 2, axis=1)

    lane_i = lax.broadcasted_iota(jnp.int32, (GW, GW), 0)
    lane_j = lax.broadcasted_iota(jnp.int32, (GW, GW), 1)
    first_j = lane_j % DH < HALF
    turn = jnp.where(
        first_j & (lane_i == lane_j + HALF),
        -1.0,
        jnp.where((~first_j) & (lane_i == lane_j - HALF), 1.0, 0.0),
    ).astype(BF)
    for copy in load_q:
        copy.wait()

    @pl.loop(0, GROUPS)
    def _(i):
        raw = q_raw[i]
        q_rot[i] = (raw.astype(F32) * cos_q() + dot(raw, turn, NN) * sin_q()).astype(BF)

    def early(j):
        rows = pl.ds(j * 512, 512)
        ag32[j] = dot(g_own[block], w_all[block, rows, :], NT)

    for copy in load_g:
        copy.wait()
    load_w.wait()
    early(0)

    halo_a.wait_recv()
    halo_b.wait_recv()

    near_index = (
        lax.broadcasted_iota(jnp.int32, (NEAR, TOK), 0) + ctx * SPAN - SPAN
    )
    allowed = (near_index >= window_ref[0:1, :]) & (near_index < window_ref[1:2, :])
    head_row = lax.broadcasted_iota(jnp.int32, (GH, NEAR, GW), 0)
    head_col = lax.broadcasted_iota(jnp.int32, (GH, NEAR, GW), 2) // DH
    own_head = head_row == head_col

    def spread(row, i):
        sl = pl.ds(pl.multiple_of(i * GW, GW), GW)
        parts = [near_kv[slot, :, sl].astype(F32)[row : row + SPAN] for slot in (1, 0, 2)]
        near = jnp.concatenate(parts, axis=0)
        wide = jnp.where(own_head, near[None], 0.0)
        return wide.reshape(GH * NEAR, GW).astype(BF)

    def gather_heads(wide):
        shaped = wide.reshape(GH, NEAR, GW)
        return jnp.sum(jnp.where(own_head, shaped, 0.0), axis=0)

    pair_a = []
    for i in range(GROUPS):
        keys = spread(0, i)
        values = spread(SPAN, i)
        keys_s[i] = keys
        values_s[i] = values
        scores = SCALE * dot(keys, q_rot[i], NT).reshape(GH, NEAR, TOK)
        masked = jnp.where(allowed[None], scores, -1e30)
        highest = jnp.max(masked, axis=1, keepdims=True)
        expo = jnp.where(allowed[None], jnp.exp(masked - highest), 0.0)
        probs = (expo / jnp.sum(expo, axis=1, keepdims=True)).reshape(GH * NEAR, TOK)
        probs_s[i] = probs
        low = probs.astype(BF)
        rows = pl.ds(i * GW, GW)
        att_t[rows, :] = dot(values, low, TN).astype(BF)
        pair_a.append(remote(att_t.at[rows], att_t_pair.at[rows], pair))

    pair_w = remote(weight_hbm, w_all.at[block], pair)
    early(1)

    far_moves = []

    def pass_on(half):
        cross[half].wait_recv()
        start = quarter * 256 + half * 128
        piece = w_all.at[far_block, pl.ds(start, 128)]
        one = w_all.at[far_block, pl.ds(start, 64)]
        two = w_all.at[far_block, pl.ds(start + 64, 64)]
        up, down = (y_step[1], y_step[-1]) if half == 0 else (z_step[2], z_step[-2])
        moves = [
            remote(piece, piece, z_step[1]),
            remote(piece, piece, z_step[-1]),
            remote(one, one, up),
            remote(two, two, down),
            remote(piece, piece, pair),
        ]
        far_moves.append(moves)

    def hand_over(half):
        for k, step in ((0, 3), (1, 1), (2, 2)):
            far_moves[half][k].wait_recv()
            if k == 2:
                far_moves[half][3].wait_recv()
            rows = pl.ds(((quarter + step) % 4) * 256 + half * 128, 128)
            piece = w_all.at[far_block, rows]
            far_moves[half].append(remote(piece, piece, pair))

    pass_on(0)

    for copy in pair_g + pair_a[:2]:
        copy.wait_recv()

    def gradient(h, part, i, store):
        cols = slice(part * 512, (part + 1) * 512)
        rows = slice(i * 512, (i + 1) * 512)
        total = dot(att_t[rows, :], g_own[2 * h + core, :, cols], NN)
        total = total + dot(att_t_pair[rows, :], g_pair[h, :, cols], NN)
        store(h, i, total.astype(BF).reshape(4, 4, 2, 16, 512))

    s1, r1 = (s1a, s1b), (r1a, r1b)
    x_cols = (slice(0, WIDE), slice(WIDE, 512))

    def store_x(h, i, total):
        for low_x in range(2):
            for k in range(2):
                s1[k][2 * h + low_x, i] = total[:, :, low_x, :, x_cols[k]]

    def store_y(h, i, total):
        for to_y in range(4):
            for k in range(2):
                s2[to_y, k, i, h] = total[:, to_y, :, :, k * 256 : k * 256 + 256]

    near = (1, 3)
    x_first = {}
    y_first = {}

    def send_x(k, slot, i):
        to = flip(x, 2 if slot == 0 else near[k], 2)
        x_first[k, slot, i] = remote(s1[k].at[to, i], r1[k].at[slot, i], x_peer[near[k] - 1])

    def send_y(k, slot, i, h=None):
        to = flip(y, 2 if slot == 0 else near[k], 2)
        piece = s2.at[to, k, i] if h is None else s2.at[to, k, i, h]
        place = r2.at[k, slot, i] if h is None else r2.at[k, slot, i, h]
        y_first.setdefault((k, slot, i), []).append(remote(piece, place, y_peer[near[k] - 1]))

    x_second = {}
    y_second = {}

    def pass_x(i):
        for k in range(2):
            to = flip(x, near[1 - k], 2)
            x_first[k, 0, i].wait_recv()
            s1[k][to, i] = (s1[k][to, i].astype(F32) + r1[k][0, i].astype(F32)).astype(BF)
            x_second[k, i] = remote(s1[k].at[to, i], r1[k].at[2, i], x_peer[near[1 - k] - 1])

    def pass_y(i):
        for k in range(2):
            to = flip(y, near[1 - k], 2)
            for copy in y_first[k, 0, i]:
                copy.wait_recv()
            s2[to, k, i] = (s2[to, k, i].astype(F32) + r2[k, 0, i].astype(F32)).astype(BF)
            y_second[k, i] = remote(s2.at[to, k, i], r2.at[k, 2, i], y_peer[near[1 - k] - 1])

    gradient(0, 1, 0, store_y)
    send_y(0, 0, 0, 0)
    send_y(1, 0, 0, 0)
    gradient(1 - xh, 0, 0, store_x)
    send_x(0, 0, 0)
    send_x(1, 0, 0)
    send_x(1, 1, 0)
    gradient(1, 1, 0, store_y)
    send_y(0, 0, 0, 1)
    send_y(1, 0, 0, 1)
    send_y(0, 1, 0)
    send_y(1, 1, 0)
    gradient(xh, 0, 0, store_x)
    send_x(0, 1, 0)
    for copy in pair_a[2:]:
        copy.wait_recv()
    gradient(1 - xh, 0, 1, store_x)
    send_x(1, 0, 1)
    send_x(0, 0, 1)
    gradient(0, 1, 1, store_y)
    gradient(1, 1, 1, store_y)
    send_y(0, 0, 1)
    send_y(1, 0, 1)
    pass_on(1)
    gradient(xh, 0, 1, store_x)
    pass_x(0)
    send_x(1, 1, 1)
    send_x(0, 1, 1)
    pass_y(0)
    send_y(0, 1, 1)
    send_y(1, 1, 1)

    pair_w.wait_recv()

    @pl.loop(0, GROUPS)
    def _(i):
        att[i] = dot(probs_s[i].astype(BF), values_s[i], TN).astype(BF)

    def project(b):
        @pl.loop(0, 2)
        def _(j):
            cols = pl.ds(pl.multiple_of(j * 512, 512), 512)
            out_cols = pl.ds(pl.multiple_of(b * WIDTH + j * 512, 512), 512)
            total = dot(att[0], w_all[b, 0:GW, cols], NN)
            for i in range(1, GROUPS):
                total = total + dot(att[i], w_all[b, i * GW : (i + 1) * GW, cols], NN)
            out_stage[:, out_cols] = total.astype(BF)

    @pl.loop(0, 2)
    def _(j):
        rows = pl.ds(pl.multiple_of(j * 512, 512), 512)
        ag32[j] += dot(g_own[pair_block], w_all[pair_block, rows, :], NT)

    project(block)
    pass_x(1)
    pass_y(1)

    y2_moves = {}
    x2_moves = {}

    def second_y(i):
        for k in range(2):
            x_first[k, 1, i].wait_recv()
            x_second[k, i].wait_recv()
        y2_moves[i] = []
        for m in (2, 1, 3, 0):
            to = flip(y, m, 2)
            for k in range(2):
                total = s1[k][x, i, :, to].astype(F32)
                for j in (1, 2):
                    total = total + r1[k][j, i, :, to].astype(F32)
                t1[i, to, :, :, x_cols[k]] = total.astype(BF)
            if m:
                y2_moves[i].append(remote(t1.at[i, to], p1.at[i, m - 1], y_peer[m - 1]))

    def second_x(i):
        for k in range(2):
            for copy in y_first[k, 1, i]:
                copy.wait_recv()
            y_second[k, i].wait_recv()
        x2_moves[i] = []
        for m in (2, 1, 3, 0):
            to = flip(x, m, 2)
            h = flip(xh, m // 2, 1)
            low_x = flip(xl, m % 2, 1)
            for k in range(2):
                total = s2[y, k, i, h, :, low_x].astype(F32)
                for j in (1, 2):
                    total = total + r2[k, j, i, h, :, low_x].astype(F32)
                t2[i, to, :, :, k * 256 : k * 256 + 256] = total.astype(BF)
            if m:
                x2_moves[i].append(remote(t2.at[i, to], p2.at[i, m - 1], x_peer[m - 1]))

    z_base = counter[0]
    counter[0] += 14

    def z_move(part, m):
        index = z_base + part * 7 + m - 1
        return pltpu.make_async_remote_copy(
            src_ref=u.at[part, flip(z, m, 3)],
            dst_ref=v.at[part, m - 1],
            send_sem=sem_s.at[index],
            recv_sem=sem_r.at[index],
            device_id=z_peer[m - 1],
            device_id_type=MESH,
        )

    def third(part, i):
        moves, mine, pieces = (y2_moves[i], t1[i, y], p1) if part == 0 else (x2_moves[i], t2[i, x], p2)
        for copy in moves:
            copy.wait_recv()
        total = mine.astype(F32)
        for m in range(3):
            total = total + pieces[i, m].astype(F32)
        u[part, 4 * i : 4 * i + 4] = total.astype(BF)
        for m in (4, 3, 5, 2, 6, 1, 7):

            @pl.when(flip(z, m, 3) // 4 == i)
            def _():
                z_move(part, m).start()

    second_y(0)
    second_x(0)
    project(pair_block)
    hand_over(0)
    hand_over(1)
    third(0, 0)
    second_y(1)
    third(1, 0)
    second_x(1)

    for half in range(2):
        for k in range(4, 8):
            far_moves[half][k].wait_recv()

    @pl.loop(0, 2)
    def _(j):
        rows = pl.ds(pl.multiple_of(j * 512, 512), 512)
        total = ag32[j] + dot(g_own[far_block], w_all[far_block, rows, :], NT)
        total = total + dot(g_own[far_pair_block], w_all[far_pair_block, rows, :], NT)
        low = total.astype(BF)
        ag[2 * j] = low[:, :GW]
        ag[2 * j + 1] = low[:, GW:]

    third(0, 1)
    third(1, 1)

    @pl.loop(0, GROUPS)
    def _(i):
        keys = keys_s[i]
        values = values_s[i]
        grads = ag[i]
        probs = probs_s[i]
        low = probs.astype(BF)
        sl = pl.ds(pl.multiple_of(i * GW, GW), GW)
        vp[:, sl] = gather_heads(dot(low, grads, NN))
        shaped = probs.reshape(GH, NEAR, TOK)
        prob_grad = dot(values, grads, NT).reshape(GH, NEAR, TOK)
        row_dot = jnp.sum(shaped * prob_grad, axis=1, keepdims=True)
        score_grad = (shaped * (prob_grad - row_dot)).reshape(GH * NEAR, TOK).astype(BF)
        turned_keys = dot(keys, turn, NN).astype(BF)
        part = SCALE * dot(score_grad, keys, TN)
        part_turned = SCALE * dot(score_grad, turned_keys, TN)
        qgrad[:, sl] = (part * cos_q() - part_turned * sin_q()).astype(BF)
        kp[:, sl] = gather_heads(SCALE * dot(score_grad, q_rot[i], NN))

    halo_out[0, 0:SPAN] = kp[2 * SPAN :, :]
    halo_out[0, SPAN:] = vp[2 * SPAN :, :]
    halo_out[1, 0:SPAN] = kp[0:SPAN, :]
    halo_out[1, SPAN:] = vp[0:SPAN, :]
    back = [
        remote(halo_out.at[0], halo_in.at[0], after),
        remote(halo_out.at[1], halo_in.at[1], before),
    ]

    project(far_block)
    project(far_pair_block)

    for copy in back:
        copy.wait_recv()
    vgrad_ref[...] = vp[SPAN : 2 * SPAN, :] + halo_in[0, SPAN:] + halo_in[1, SPAN:]
    key_total = kp[SPAN : 2 * SPAN, :] + halo_in[0, 0:SPAN] + halo_in[1, 0:SPAN]
    kgrad_ref[...] = key_total * cos_k - turned(key_total) * sin_k

    for part in range(2):
        for m in range(1, 8):
            z_move(part, m).wait_recv()
    for part in range(2):
        total = u[part, z].astype(F32)
        for m in range(7):
            total = total + v[part, m].astype(F32)
        wgrad_ref[:, part * 512 : part * 512 + 512] = total * factor

    for copy in started:
        copy.wait_send()
    for part in range(2):
        for m in range(1, 8):
            z_move(part, m).wait_send()


def finish(*refs):
    sems = refs[10]
    copies = [pltpu.make_async_copy(refs[i], refs[5 + i], sems.at[i]) for i in range(5)]
    for copy in copies:
        copy.start()
    for copy in copies:
        copy.wait()


def local(video_query, audio_key, audio_value, out_weight, grad_out, query_time, window):
    factor = 1.0 / math.sqrt(TOK * lax.axis_size("ctx") * lax.axis_size("fsdp"))

    vmem = pl.BlockSpec(memory_space=pltpu.VMEM)
    hbm = pl.BlockSpec(memory_space=pltpu.HBM)
    n_sems = 88
    results = [
        ((TOK, 4 * WIDTH), BF),
        ((TOK, WIDTH), BF),
        ((SPAN, WIDTH), F32),
        ((SPAN, WIDTH), F32),
        ((16, WIDTH), F32),
    ]

    inputs = (
        video_query[0],
        jnp.concatenate([audio_key[0], audio_value[0]], axis=0),
        out_weight,
        grad_out[0],
        query_time.reshape(1, TOK),
        window,
    )

    def body(*refs):
        kernel(factor, *refs)

    outs = pl.pallas_call(
        body,
        name="fused",
        out_shape=[pltpu.VMEM(shape, dtype) for shape, dtype in results],
        in_specs=[hbm] * 6,
        out_specs=[vmem] * 5,
        scratch_shapes=[
            pltpu.VMEM((2 * SPAN, WIDTH), BF),
            pltpu.VMEM((1, TOK), jnp.int32),
            pltpu.VMEM((2, TOK), jnp.int32),
            pltpu.VMEM((GROUPS, TOK, GW), BF),
            pltpu.VMEM((GROUPS, TOK, GW), BF),
            pltpu.VMEM((3, 2 * SPAN, WIDTH), BF),
            pltpu.VMEM((4, WIDTH, WIDTH), BF),
            pltpu.VMEM((4, TOK, WIDTH), BF),
            pltpu.VMEM((2, TOK, WIDTH), BF),
            pltpu.VMEM((GROUPS, GH * NEAR, GW), BF),
            pltpu.VMEM((GROUPS, GH * NEAR, GW), BF),
            pltpu.VMEM((GROUPS, GH * NEAR, TOK), F32),
            pltpu.VMEM((GROUPS, TOK, GW), BF),
            pltpu.VMEM((WIDTH, TOK), BF),
            pltpu.VMEM((WIDTH, TOK), BF),
            pltpu.VMEM((2, TOK, 512), F32),
            pltpu.VMEM((GROUPS, TOK, GW), BF),
            pltpu.VMEM((TOK, 256), F32),
            pltpu.VMEM((NEAR, WIDTH), F32),
            pltpu.VMEM((NEAR, WIDTH), F32),
            pltpu.VMEM((2, 2 * SPAN, WIDTH), F32),
            pltpu.VMEM((2, 2 * SPAN, WIDTH), F32),
            pltpu.VMEM((4, 2, 4, 4, 16, WIDE), BF),
            pltpu.VMEM((4, 2, 4, 4, 16, 512 - WIDE), BF),
            pltpu.VMEM((3, 2, 4, 4, 16, WIDE), BF),
            pltpu.VMEM((3, 2, 4, 4, 16, 512 - WIDE), BF),
            pltpu.VMEM((4, 2, 2, 2, 4, 2, 16, 256), BF),
            pltpu.VMEM((2, 3, 2, 2, 4, 2, 16, 256), BF),
            pltpu.VMEM((2, 4, 4, 16, 512), BF),
            pltpu.VMEM((2, 3, 4, 16, 512), BF),
            pltpu.VMEM((2, 4, 4, 16, 512), BF),
            pltpu.VMEM((2, 3, 4, 16, 512), BF),
            pltpu.VMEM((2, 8, 16, 512), BF),
            pltpu.VMEM((2, 7, 16, 512), BF),
            pltpu.SemaphoreType.DMA((24,)),
            pltpu.SemaphoreType.DMA((n_sems,)),
            pltpu.SemaphoreType.DMA((n_sems,)),
        ],
        compiler_params=pltpu.CompilerParams(
            collective_id=0, has_side_effects=True, vmem_limit_bytes=46 << 20
        ),
    )(
        *[pltpu.with_memory_space_constraint(arg, pltpu.HBM) for arg in inputs]
    )
    outs = pl.pallas_call(
        finish,
        name="finish",
        out_shape=[jax.ShapeDtypeStruct(shape, dtype) for shape, dtype in results],
        in_specs=[vmem] * 5,
        out_specs=[hbm] * 5,
        scratch_shapes=[pltpu.SemaphoreType.DMA((5,))],
        compiler_params=pltpu.CompilerParams(vmem_limit_bytes=4 << 20),
    )(*[pltpu.with_memory_space_constraint(out, pltpu.VMEM) for out in outs])
    output, query_grad, key_grad, value_grad, weight_grad = outs
    return (output[None], query_grad[None], key_grad[None], value_grad[None], weight_grad)


def solution(mesh):
    in_specs = (
        P("fsdp", "ctx", None),
        P("fsdp", "ctx", None),
        P("fsdp", "ctx", None),
        P(None, "fsdp"),
        P("fsdp", "ctx", None),
        P("ctx"),
        P(None, "ctx"),
    )
    out_specs = (
        P("fsdp", "ctx", None),
        P("fsdp", "ctx", None),
        P("fsdp", "ctx", None),
        P("fsdp", "ctx", None),
        P("ctx", "fsdp"),
    )
    return jax.shard_map(local, mesh=mesh, in_specs=in_specs, out_specs=out_specs, check_vma=False)
```
